512 devices in a mesh: gx: 16 (over x, y), gy: 32 (over z, core).
Axes of the slice: x: 4, y: 4, z: 16, core: 2. Of those that a mesh axis runs over, the one named last changes fastest.
Arguments:
- residual: bfloat16 [64, 6144], P('gy', 'gx')
- attn_gain: float32 [6144], P('gx'), may hold values from 0.25 to 1.75
- wqkv: bfloat16 [6144, 8192], P('gx', 'gy'), may hold values from -0.078125 to 0.078125
- rotated_key_cache: bfloat16 [64, 2048, 1024], P('gx', 'gy'), may hold values from -6 to 6
- slot_value_cache: bfloat16 [64, 2048, 1024], P('gx', 'gy'), may hold values from -6 to 6
- lengths: int32 [64], P('gx'), may hold values from 0 to 8191
- starts: int32 [64], P('gx'), may hold values from 0 to 8191, as said below
- wo: bfloat16 [6144, 6144], P('gy', 'gx')
- post_gain: float32 [6144], P('gx'), may hold values from 0.25 to 1.75
- moe_gain: float32 [6144], P('gx'), may hold values from 0.25 to 1.75
- router: bfloat16 [6144, 8], P('gx'), may hold values from -0.15625 to 0.15625
- expert_ids: int32 [64, 2], replicated, may hold values from 0 to 7, all different within a row; in each aligned block of 64 rows (0 to 63, 64 to 127, ...) at most 32 rows name the same one
- w_gate_up: bfloat16 [2, 6144, 2, 16384], P(None, 'gx', None, 'gy'), may hold values from -0.078125 to 0.078125
- w_down: bfloat16 [2, 16384, 6144], P(None, 'gy', 'gx'), may hold values from -0.1875 to 0.1875
Outputs:
- mixed: bfloat16 [64, 6144], P('gy', 'gx')
- expert_out: bfloat16 [64, 6144], P('gy', 'gx')
The draws below stay inside these ranges and needn't reach their ends.
Inputs may be any that keep to these rules, and one draw needn't show every extreme that they name: `starts`: each start is at most its request's length. `expert_ids`: the 2 experts of a request differ; no expert is named by more than 32 requests, a bound that some block reaches.
All inputs are finite; a program needn't handle non-finite values.
Results may differ from the reference program's by a relative error of at most 0.025.
Values may be sent and summed in bfloat16 or wider, within the bound.
A program may use at most 64 MiB of HBM per device.

```python
import math
import jax
import jax.numpy as jnp
import numpy as np
from jax import lax

MODEL_WIDTH = 6144
QUERY_HEADS = 48
KEY_VALUE_HEADS = 8
HEAD_SIZE = 128
NEXP = 8
TOPK = 2
WINDOW_SLOTS = 2048
FF_WIN = 16384
EXP_WIN = 2
REQUEST_TOTAL = 64
CAP = 32


def draw_residual(key, part):
    key = jax.random.fold_in(key, 3)
    noise_key, row_key = jax.random.split(key, 2)
    columns = jnp.exp(jnp.linspace(math.log(0.55), math.log(1.75), MODEL_WIDTH, dtype=jnp.float32))
    row_scale = jnp.exp(jax.random.uniform(row_key, (REQUEST_TOTAL, 1), jnp.float32, math.log(0.3), math.log(3.0)))
    sample = jax.random.normal(noise_key, (REQUEST_TOTAL, MODEL_WIDTH), jnp.float32)
    return (sample * row_scale * columns[None, :]).astype(jnp.bfloat16)


def draw_wo(key, part):
    key = jax.random.fold_in(key, 5)
    columns = jnp.exp(jnp.linspace(math.log(0.5), math.log(1.5), MODEL_WIDTH, dtype=jnp.float32))
    sample = jax.random.normal(key, (QUERY_HEADS * HEAD_SIZE, MODEL_WIDTH), jnp.float32)
    return (sample * columns[None, :] * (QUERY_HEADS * HEAD_SIZE) ** (-0.5)).astype(jnp.bfloat16)


def cache_bounds(key):
    key = jax.random.fold_in(key, 7)
    length_key, spot_key, cut_key, open_key = jax.random.split(key, 4)
    lengths = jax.random.randint(length_key, (REQUEST_TOTAL,), 0, 4 * WINDOW_SLOTS, dtype=jnp.int32)
    spots = jax.random.permutation(spot_key, REQUEST_TOTAL)
    lengths = lengths.at[spots[0]].set(4 * WINDOW_SLOTS - 1).at[spots[1]].set(0)
    cuts = jax.random.randint(cut_key, (REQUEST_TOTAL,), 0, lengths + 1, dtype=jnp.int32)
    opened = jax.random.randint(open_key, (REQUEST_TOTAL,), 0, 2, dtype=jnp.int32)
    starts = jnp.where(opened == 0, 0, cuts).astype(jnp.int32)
    starts = starts.at[spots[0]].set(4 * WINDOW_SLOTS - 1).at[spots[1]].set(0)
    return (lengths, starts)


def draw_lengths(key, part):
    return cache_bounds(key)[0]


def draw_starts(key, part):
    return cache_bounds(key)[1]


def levels(own_key, dims, cuts, smallest, high):
    def one(dim, blocks):
        draws = jax.random.uniform(jax.random.fold_in(jax.random.fold_in(own_key, 6), dim), (blocks,), jnp.float32, smallest / len(cuts), high / len(cuts))
        return jnp.repeat(jnp.exp(draws), dims[dim] // blocks).reshape((-1,) + (1,) * (len(dims) - dim - 1))

    level = one(*cuts[0])
    for cut in cuts[1:]:
        level = level * one(*cut)
    return level


def shared_out(rng, own, number, rows, count, top, bound, skew):
    order = jax.random.permutation(rng, count)
    packed, usual = shares(count, rows * top, bound, skew, True), shares(count, rows * top, bound, skew, False)
    places = jnp.arange(count)

    def named(tallies, rotation):
        used = int((tallies > 0).sum())
        fixed = max(1, used // 4)
        moved = fixed + (places - fixed + rotation * (used - fixed)) % max(1, count - fixed)
        return jnp.zeros((count,), jnp.int32).at[order[jnp.where(places < fixed, places, moved)]].set(jnp.asarray(tallies, jnp.int32))

    tallies = jnp.where(number % 4 == 0, named(packed, number // 4), named(usual, number - number // 4 - 1))
    mixed = jax.random.permutation(jax.random.fold_in(own, 3), count)
    source_of, receiver = mixed[0:count // 2 * 2:2], mixed[1:count // 2 * 2:2]
    slack = jnp.minimum(tallies[source_of] - 1, bound - tallies[receiver]) // 2
    slack = jnp.where((source_of == order[0]) | (receiver == order[0]) | (tallies[receiver] == 0), 0, jnp.maximum(slack, 0))
    moved = jax.random.randint(jax.random.fold_in(own, 4), (count // 2,), 0, 1 << 20) % (slack + 1)
    tallies = tallies.at[source_of].add(-moved).at[receiver].add(moved)
    members = jnp.searchsorted(jnp.cumsum(tallies), jnp.arange(rows * top), side="right").astype(jnp.int32)
    grid = members.reshape(top, rows).T
    grid = grid[jax.random.permutation(jax.random.fold_in(own, 1), rows)]
    rotation = jax.random.randint(jax.random.fold_in(own, 2), (rows, 1), 0, top)
    return jnp.take_along_axis(grid, (jnp.arange(top)[None, :] + rotation) % top, axis=1)


def shares(amount, total, most, lean, full):
    weights = [(1 << 20) // math.isqrt(grade ** lean) + 1 for grade in range(1, amount + 1)]
    largest = most if full else min(most, max(-(-total // amount), total * weights[0] // sum(weights)))
    least = 1 if total - largest >= amount - 1 else 0
    given, spare = [largest] + [least] * (amount - 1), total - largest - least * (amount - 1)
    while spare > 0:
        free = [i for i in range(1, amount) if given[i] < largest] or [i for i in range(1, amount) if given[i] < most]
        mass, remaining = sum([weights[i] for i in free]), spare
        for i in free:
            extra = min(most - given[i], max(1, remaining * weights[i] // mass), spare)
            given[i] = given[i] + extra
            spare = spare - extra
    return np.array(given)


def normal_values(key, extent, spread, reach, shards=(), kind=jnp.bfloat16):
    drawn = spread * jax.random.normal(key, extent, jnp.float32)
    if shards:
        drawn = drawn * levels(key, extent, shards, -0.22, 0.18)
    return jnp.clip(drawn, -reach, reach).astype(kind)


def setup_inputs(seed: int = 0) -> dict:
    keys = jax.random.split(jax.random.key(seed), 15)
    residual = draw_residual(jax.random.fold_in(keys[14], 71), 0)
    attn_gain = jnp.clip(1.0 + 0.15 * jax.random.normal(keys[1], (MODEL_WIDTH,), jnp.float32), 0.25, 1.75)
    wqkv = normal_values(keys[2], (MODEL_WIDTH, (QUERY_HEADS + 2 * KEY_VALUE_HEADS) * HEAD_SIZE), MODEL_WIDTH ** -0.5, 0.078125, ((0, 16), (1, 32)))
    rotated_key_cache = normal_values(keys[3], (REQUEST_TOTAL, WINDOW_SLOTS, KEY_VALUE_HEADS * HEAD_SIZE), 1.0, 6.0, ((0, 16), (1, 32)))
    slot_value_cache = normal_values(keys[4], (REQUEST_TOTAL, WINDOW_SLOTS, KEY_VALUE_HEADS * HEAD_SIZE), 1.0, 6.0, ((0, 16), (1, 32)))
    lengths = draw_lengths(jax.random.fold_in(keys[14], 71), 0)
    starts = draw_starts(jax.random.fold_in(keys[14], 71), 0)
    wo = draw_wo(jax.random.fold_in(keys[14], 71), 0)
    post_gain = jnp.clip(1.0 + 0.15 * jax.random.normal(keys[8], (MODEL_WIDTH,), jnp.float32), 0.25, 1.75)
    moe_gain = jnp.clip(1.0 + 0.15 * jax.random.normal(keys[9], (MODEL_WIDTH,), jnp.float32), 0.25, 1.75)
    router = normal_values(keys[10], (MODEL_WIDTH, NEXP), (MODEL_WIDTH // 4) ** -0.5, 0.15625, ((0, 16),))
    expert_ids_keys = jax.random.split(jax.random.fold_in(keys[11], 1), REQUEST_TOTAL // REQUEST_TOTAL)
    expert_ids_turns = jax.random.permutation(jax.random.fold_in(keys[11], 3), REQUEST_TOTAL // REQUEST_TOTAL)
    expert_ids = jax.vmap(lambda own, number: shared_out(jax.random.fold_in(keys[11], 2), own, number, REQUEST_TOTAL, NEXP, TOPK, CAP, 1))(expert_ids_keys, expert_ids_turns).reshape((REQUEST_TOTAL, TOPK))
    w_gate_up = normal_values(keys[12], (EXP_WIN, MODEL_WIDTH, 2, FF_WIN), MODEL_WIDTH ** -0.5, 0.078125, ((1, 16), (3, 32)))
    w_down = normal_values(keys[13], (EXP_WIN, FF_WIN, MODEL_WIDTH), (FF_WIN // 16) ** -0.5, 0.1875, ((1, 32), (2, 16)))
    return {"residual": residual, "attn_gain": attn_gain, "wqkv": wqkv, "rotated_key_cache": rotated_key_cache, "slot_value_cache": slot_value_cache, "lengths": lengths, "starts": starts, "wo": wo, "post_gain": post_gain, "moe_gain": moe_gain, "router": router, "expert_ids": expert_ids, "w_gate_up": w_gate_up, "w_down": w_down}


epsilon = 1e-05
score_cap = 30.0

def rms_scale(values):
    return lax.rsqrt(lax.optimization_barrier(jnp.mean(values * values, axis=-1, keepdims=True)) + epsilon)

def rotary_position_rotate(blocks, positions):
    half_width = blocks.shape[-1] // 2
    frequency = 10000.0 ** (-(jnp.arange(half_width, dtype=jnp.float32) * 2.0 / blocks.shape[-1]))
    angles = positions.astype(jnp.float32)[:, None] * frequency[None, :]
    cosine = jnp.cos(angles)[:, None, :]
    sine_part = jnp.sin(angles)[:, None, :]
    leading = blocks[..., :half_width]
    trailing = blocks[..., half_width:]
    return jnp.concatenate([leading * cosine - trailing * sine_part, trailing * cosine + leading * sine_part], axis=-1)

def attend_one(inputs):
    query_rows, fresh_key, fresh_value, stored_keys, stored_values, length, window_start = inputs
    query_group_width = QUERY_HEADS // KEY_VALUE_HEADS
    logit_scale_factor = HEAD_SIZE ** (-0.5)
    query_rows = query_rows.astype(jnp.float32).reshape(KEY_VALUE_HEADS, query_group_width, HEAD_SIZE)
    stored_keys = stored_keys.astype(jnp.float32).reshape(WINDOW_SLOTS, KEY_VALUE_HEADS, HEAD_SIZE)
    stored_values = stored_values.astype(jnp.float32).reshape(WINDOW_SLOTS, KEY_VALUE_HEADS, HEAD_SIZE)
    scores = jnp.einsum('hgd,shd->hgs', query_rows, stored_keys) * logit_scale_factor
    scores = score_cap * jnp.tanh(scores / score_cap)
    slot_index = jnp.arange(WINDOW_SLOTS, dtype=jnp.int32)
    position = length - 1 - jnp.mod(length - 1 - slot_index, WINDOW_SLOTS)
    lowest = jnp.maximum(window_start, length - WINDOW_SLOTS + 1)
    usable = position >= lowest
    weights = jnp.where(usable[None, None, :], jnp.exp(scores), 0.0)
    rounded = lax.optimization_barrier(weights.astype(jnp.bfloat16)).astype(jnp.float32)
    weighted_value_sum = jnp.einsum('hgs,shd->hgd', rounded, stored_values)
    denominator = lax.optimization_barrier(jnp.sum(weights, axis=-1))
    self_score = jnp.einsum('cqm,cm->cq', query_rows, fresh_key.astype(jnp.float32).reshape(KEY_VALUE_HEADS, HEAD_SIZE)) * logit_scale_factor
    own_weight = jnp.exp(score_cap * jnp.tanh(self_score / score_cap))
    self_score_rounded = lax.optimization_barrier(own_weight.astype(jnp.bfloat16)).astype(jnp.float32)
    weighted_value_sum = weighted_value_sum + self_score_rounded[..., None] * fresh_value.astype(jnp.float32).reshape(KEY_VALUE_HEADS, 1, HEAD_SIZE)
    denominator = denominator + own_weight
    return (weighted_value_sum / denominator[..., None]).reshape(QUERY_HEADS * HEAD_SIZE).astype(jnp.bfloat16)

def reference(residual, attn_gain, wqkv, rotated_key_cache, slot_value_cache, lengths, starts, wo, post_gain, moe_gain, router, expert_ids, w_gate_up, w_down):
    stream = residual.astype(jnp.float32)
    normed = (stream * rms_scale(stream) * attn_gain).astype(jnp.bfloat16)
    query_key_value_sums = jnp.dot(normed, wqkv, preferred_element_type=jnp.float32)
    head_block_list = query_key_value_sums.reshape(REQUEST_TOTAL, QUERY_HEADS + 2 * KEY_VALUE_HEADS, HEAD_SIZE)
    rotated_input = rotary_position_rotate(head_block_list[:, :QUERY_HEADS + KEY_VALUE_HEADS], lengths)
    head_block_list = jnp.concatenate([rotated_input, head_block_list[:, QUERY_HEADS + KEY_VALUE_HEADS:]], axis=1).astype(jnp.bfloat16)
    query_rows = head_block_list[:, :QUERY_HEADS].reshape(REQUEST_TOTAL, QUERY_HEADS * HEAD_SIZE)
    fresh_key = head_block_list[:, QUERY_HEADS:QUERY_HEADS + KEY_VALUE_HEADS].reshape(REQUEST_TOTAL, KEY_VALUE_HEADS * HEAD_SIZE)
    fresh_value = head_block_list[:, QUERY_HEADS + KEY_VALUE_HEADS:].reshape(REQUEST_TOTAL, KEY_VALUE_HEADS * HEAD_SIZE)
    attended = lax.map(attend_one, (query_rows, fresh_key, fresh_value, rotated_key_cache, slot_value_cache, lengths, starts))
    branch = jnp.dot(attended, wo, preferred_element_type=jnp.float32)
    stream_mid = stream + branch * rms_scale(branch) * post_gain
    moe_input = stream_mid * rms_scale(stream_mid) * moe_gain
    logits = jnp.dot(moe_input, router.astype(jnp.float32), precision=lax.Precision.HIGHEST)
    exponent = jnp.exp(logits)
    chances = exponent / lax.optimization_barrier(jnp.sum(exponent, axis=-1, keepdims=True))
    window = jnp.arange(EXP_WIN, dtype=jnp.int32)
    chosen = jnp.any(expert_ids[:, :, None] == window[None, None, :], axis=1)
    combine = jnp.where(chosen, chances[:, :EXP_WIN], 0.0).astype(jnp.bfloat16)
    moe_rows = moe_input.astype(jnp.bfloat16)
    expert_sum = jnp.zeros((REQUEST_TOTAL, MODEL_WIDTH), jnp.float32)
    for expert in range(EXP_WIN):
        gate_up = jnp.dot(moe_rows, w_gate_up[expert].reshape(MODEL_WIDTH, 2 * FF_WIN), preferred_element_type=jnp.float32)
        gate_up = gate_up.reshape(REQUEST_TOTAL, 2, FF_WIN)
        hidden = (jax.nn.gelu(gate_up[:, 0], approximate=True) * gate_up[:, 1]).astype(jnp.bfloat16)
        expert_sum = expert_sum + combine[:, expert:expert + 1].astype(jnp.float32) * jnp.dot(hidden, w_down[expert], preferred_element_type=jnp.float32)
    return (stream_mid.astype(jnp.bfloat16), expert_sum.astype(jnp.bfloat16))
```

```python
import functools
import math

import jax
import jax.numpy as jnp
from jax import lax
from jax.experimental import pallas as pl
from jax.experimental.pallas import tpu as pltpu
from jax.sharding import PartitionSpec as P

MODEL_WIDTH = 6144
QUERY_HEADS = 48
KEY_VALUE_HEADS = 8
HEAD_SIZE = 128
WINDOW_SLOTS = 2048
EXP_WIN = 2
NX, NY = 16, 32
EPS = 1e-05
CAP = 30.0
F32, BF16, I32 = jnp.float32, jnp.bfloat16, jnp.int32
MESH = pl.DeviceIdType.MESH

ST_B, ST_C, ST_D, ST_E, ST_F, ST_G, ST_J, ST_A, ST_K, ST_H, ST_L = range(11)


def iota(shape, dim):
    return lax.broadcasted_iota(I32, shape, dim)


def onehot(condition):
    return jnp.where(condition, 1.0, 0.0).astype(BF16)


def mm(a, b):
    return jnp.dot(a, b, preferred_element_type=F32)


def pick(number, values):
    result = values[-1]
    for k in range(len(values) - 2, -1, -1):
        result = jnp.where(number == k, values[k], result)
    return result


def gain_tile(row):
    s = iota((8, 128), 0)
    parts = [jnp.broadcast_to(row[:, 128 * c : 128 * c + 128], (8, 128)) for c in range(3)]
    return pick(s >> 1, parts + [jnp.ones((8, 128), F32)])


def fold_requests(v):
    u = v + pltpu.roll(v, 4, 0)
    return u + pltpu.roll(u, 2, 0)


def split_terms(v):
    hi = v.astype(BF16).astype(F32)
    rest = v - hi
    mid = rest.astype(BF16).astype(F32)
    low = rest - mid
    return hi + pltpu.roll(mid, 16, 1) + pltpu.roll(low, 32, 1)


def join_terms(v):
    return v + pltpu.roll(v, 112, 1) + pltpu.roll(v, 96, 1)


def as_rows(tile):
    return jnp.concatenate([tile[0:2], tile[2:4], tile[4:6]], axis=1)


def kernel(
    residual, attn_gain, wqkv, keys, values, lengths, starts, wo, post_gain, moe_gain, router, ids, w_gate_up, w_down,
    mixed_ref, out_ref,
    v_res, v_ag, v_pg, v_mg, v_rt, v_ids, v_wqkv, v_keys, v_vals, v_wo, v_gu, v_wd, w_split,
    perm_c, sel_e, sel_g, perm_k, perm_l, rm, mask, base_t, branch_t, q_rows, x_moe,
    t_b, r_b, s_c, r_c, t_d, r_d, s_e, r_e, t_f, r_f, s_g, r_g, t_j, r_j, s_a, r_a, s_k, r_k, t_h, r_h, s_l, r_l,
    load_sem, send_sem, recv_sem,
):
    gx = lax.axis_index("gx")
    gy = lax.axis_index("gy")
    z, core = lax.div(gy, 2), lax.rem(gy, 2)
    px, py = lax.div(gx, 4), lax.rem(gx, 4)

    loads = []

    def load(src, dst, k):
        c = pltpu.make_async_copy(src, dst, load_sem.at[k])
        c.start()
        loads.append(c)

    load(residual, v_res, 0)
    load(attn_gain, v_ag, 1)
    load(post_gain, v_pg, 2)
    load(moe_gain, v_mg, 3)
    load(router, v_rt, 4)
    load(ids, v_ids, 5)
    load(wqkv, v_wqkv, 6)
    load(keys, v_keys, 7)
    load(values, v_vals, 8)
    load(wo.at[pl.ds(pl.multiple_of(64 * core, 64), 128)], v_wo.at[pl.ds(0, 128)], 9)
    load(
        wo.at[pl.ds(pl.multiple_of(128 * (1 - core), 64), 64)],
        v_wo.at[pl.ds(pl.multiple_of(128 + 64 * core, 64), 64)],
        10,
    )
    load(w_gate_up, v_gu, 11)
    load(w_down, v_wd, 12)

    def over_gy(act):
        def body(q, carry):
            h = lax.div(q + 1, 2)
            far = lax.rem(z + 8 + h * (1 - 2 * lax.rem(q, 2)), 16)
            act(2 * far + core)
            act(2 * far + 1 - core)
            return carry

        lax.fori_loop(0, 15, body, 0)
        act(2 * z + 1 - core)

    def over_gx(act):
        def shift(t):
            return lax.rem(10 - lax.div(t * (t + 1), 2), 4)

        def body(k, carry):
            qx = lax.rem(px + shift(lax.div(k, 4)), 4)
            qy = lax.rem(py + shift(lax.rem(k, 4)), 4)
            act(4 * qx + qy)
            return carry

        lax.fori_loop(0, 15, body, 0)

    barrier = pltpu.get_barrier_semaphore()
    over_gy(lambda p: pl.semaphore_signal(barrier, inc=1, device_id=(gx, p), device_id_type=MESH))
    over_gx(lambda p: pl.semaphore_signal(barrier, inc=1, device_id=(p, gy), device_id_type=MESH))

    def send(stage, along, src, dst, each):
        me = gy if along == "gy" else gx

        def act(p):
            pltpu.make_async_remote_copy(
                src_ref=src.at[p] if each else src,
                dst_ref=dst.at[me],
                send_sem=send_sem.at[stage],
                recv_sem=recv_sem.at[stage],
                device_id=(gx, p) if along == "gy" else (p, gy),
                device_id_type=MESH,
            ).start()

        (over_gy if along == "gy" else over_gx)(act)
        dst[me] = src[me] if each else src[...]

    def peers_of(dst):
        return dst.at[pl.ds(0, dst.shape[0] - 1)]

    def received(stage, dst):
        pltpu.make_async_copy(peers_of(dst), peers_of(dst), recv_sem.at[stage]).wait()

    def total(ref):
        return jnp.sum(ref[...].astype(F32), axis=0)

    s8, l8 = iota((8, 128), 0), iota((8, 128), 1)
    for c in loads[:6]:
        c.wait()
    res = v_res[...].astype(F32)
    base = jnp.concatenate([res[:, 0:128], res[:, 128:256], res[:, 256:384], jnp.zeros((2, 128), F32)], axis=0)
    base_t[...] = base
    ag, pg, mg = gain_tile(v_ag[...]), gain_tile(v_pg[...]), gain_tile(v_mg[...])
    rt = v_rt[...].astype(F32)
    for e in range(8):
        row = rt[e : e + 1]
        parts = [jnp.broadcast_to(row[:, 128 * c : 128 * c + 128], (8, 128)) for c in range(3)]
        rm[e] = pick(s8 >> 1, parts + [jnp.zeros((8, 128), F32)]) * mg

    def lane_sums(terms):
        acc = jnp.zeros((8, 128), F32)
        for k, term in terms:
            acc = jnp.where(l8 == k, jnp.sum(term, axis=1, keepdims=True), acc)
        return fold_requests(acc)

    base_sums = lane_sums([(0, base * base)] + [(3 + e, base * rm[e]) for e in range(8)])
    t_b[...] = jnp.where(s8 < 6, base, split_terms(base_sums)).astype(BF16)

    row, lane = iota((512, 256), 0), iota((512, 256), 1)
    n = 4 * ((row >> 3) & 15) + (row & 3)
    perm_c[...] = onehot(lane == ((n >> 1) << 3) + 2 * (row >> 7) + (n & 1))

    pl.semaphore_wait(barrier, NX + NY - 2)
    send(ST_B, "gy", t_b, r_b, False)

    row, lane = iota((256, 256), 0), iota((256, 256), 1)
    j, t = row >> 3, (row >> 2) & 1
    head = 3 * (j >> 1) + jnp.where(t == 1, 1, 2 * (j & 1))
    sel_e[...] = onehot(lane == ((head >> 1) << 3) + ((head & 1) << 2) + (row & 3))

    row, lane = iota((512, 128), 0), iota((512, 128), 1)
    s = row & 7
    n = 2 * ((row >> 3) & 31) + (s & 1)
    sel_g[...] = onehot((lane == ((n >> 2) << 3) + ((row >> 8) << 2) + (n & 3)) & (s < 6))

    lane_code, row_code = [], []
    id_rows = v_ids[...]
    for e in range(EXP_WIN):
        picked = jnp.where((id_rows[0:1] == e) | (id_rows[1:2] == e), 1.0, 0.0)
        a, b = iota((64, 64), 0), iota((64, 64), 1)
        column = jnp.sum(jnp.where(a == b, picked, 0.0), axis=1, keepdims=True)
        a, b = iota((64, 256), 0), iota((64, 256), 1)
        of = 2 * (b >> 3) + (b & 1)
        before = jnp.sum(jnp.where(a < of, column, 0.0), axis=0, keepdims=True)
        named = jnp.sum(jnp.where(a == of, column, 0.0), axis=0, keepdims=True)
        lane_code.append(jnp.where(named > 0.5, before, -1.0))
        a, b = iota((256, 64), 0), iota((256, 64), 1)
        of = 2 * (a >> 3) + (a & 1)
        before = jnp.sum(jnp.where(b < of, picked, 0.0), axis=1, keepdims=True)
        named = jnp.sum(jnp.where(b == of, picked, 0.0), axis=1, keepdims=True)
        row_code.append(jnp.where(named > 0.5, before, -1.0))

    row, lane = iota((128, 256), 0), iota((128, 256), 1)
    q, s = row & 7, lane & 7
    slot = (2 * (row >> 3) + (row & 1)).astype(F32)
    for e in range(EXP_WIN):
        here = slot == lane_code[e]
        for c in range(3):
            perm_k[pl.ds((3 * e + c) * 128, 128)] = onehot(here & ((s >> 1) == c))
    sums_here = (
        ((q >> 1) == 0) & (slot == lane_code[0]) | ((q >> 1) == 1) & (slot == lane_code[1])
    ) & ((s >> 1) == 3)
    own = ((q >> 1) == 2) & (lane == 8 * gy + 6 + (q & 1))
    perm_k[pl.ds(768, 128)] = onehot(sums_here | own)

    row, lane = iota((256, 256), 0), iota((256, 256), 1)
    slot = (2 * (lane >> 4) + (lane & 1)).astype(F32)
    for e in range(EXP_WIN):
        here = (slot == row_code[e]) & (((lane >> 3) & 1) == e) & ((row & 7) < 6)
        for ct in range(4):
            perm_l[pl.ds((4 * e + ct) * 256, 256)] = onehot(here & (((lane >> 1) & 3) == ct))

    row, lane = iota((8, 256), 0), iota((8, 256), 1)
    last = pick(lane >> 6, [lengths[r] for r in range(4)]) - 1
    first = pick(lane >> 6, [starts[r] for r in range(4)])
    position = last - ((last - (64 * gy + (lane & 63))) & (WINDOW_SLOTS - 1))
    usable = (position >= jnp.maximum(first, last - (WINDOW_SLOTS - 2))) & ((lane >> 6) == (row & 3))
    mask[...] = jnp.where(usable, 1.0, 0.0)

    turn = (l8 & 63).astype(F32)
    angle = pick(s8 & 3, [lengths[r] for r in range(4)]).astype(F32) * jnp.exp(turn * (-2.0 * math.log(10000.0) / 128))
    rotated = 2 * gy < QUERY_HEADS + KEY_VALUE_HEADS
    cosine = jnp.where(rotated, jnp.cos(angle), 1.0)
    sine = jnp.where(rotated, jnp.where(l8 < 64, -1.0, 1.0) * jnp.sin(angle), 0.0)

    v_wo[pl.ds(pl.multiple_of(192 - 64 * core, 64), 64)] = jnp.zeros((64, 384), BF16)
    loads[6].wait()

    received(ST_B, r_b)
    x = r_b[...].astype(F32)
    rows = mm(perm_c[...], (x * ag).reshape(256, 128).astype(BF16))
    left = jnp.concatenate([rows[128 * c : 128 * c + 128] for c in range(3)], axis=1).astype(BF16)
    sums = mm(left, v_wqkv[...])
    hh = (iota((128, 128), 0) >> 2) & 1
    sums = jnp.where(hh == 0, sums[:, 0:128], sums[:, 128:256])
    s_c[...] = jnp.concatenate([sums.reshape(16, 8, 128), rows[384:512].reshape(16, 8, 128)], axis=1).astype(BF16)
    send(ST_C, "gx", s_c, r_c, True)
    x_moe[...] = (x * mg).reshape(256, 128).astype(BF16)
    for c in loads[11:12]:
        c.wait()
    for e in range(EXP_WIN):
        for u in range(2):
            w_split[e, u] = v_gu[e, :, u, :]

    received(ST_C, r_c)
    both = total(r_c)
    square = join_terms(both[8:16])
    scale = lax.rsqrt(square[:, 0:1] / MODEL_WIDTH + EPS)
    heads = both[0:8] * scale
    heads = heads * cosine + pltpu.roll(heads, 64, 1) * sine
    t_d[...] = heads.astype(BF16)
    send(ST_D, "gy", t_d, r_d, False)

    def gate_up(x_rows, out):
        rows = mm(perm_k[...], x_rows)
        rows16 = rows.astype(BF16)
        ct = (iota((128, 128), 0) & 7) >> 1
        for e in range(EXP_WIN):
            left = jnp.concatenate([rows16[(3 * e + c) * 128 : (3 * e + c) * 128 + 128] for c in range(3)], axis=1)
            halves = []
            for u in range(2):
                full = mm(left, w_split[e, u])
                halves.append(pick(ct, [full[:, 128 * k : 128 * k + 128] for k in range(4)]).reshape(16, 8, 128))
            out[:, pl.ds(16 * e, 16), :] = jnp.concatenate(halves, axis=1).astype(BF16)
        sums = rows[768:896].reshape(16, 8, 128)
        out[:, pl.ds(32, 16), :] = jnp.concatenate([sums, jnp.zeros((16, 8, 128), F32)], axis=1).astype(BF16)

    gate_up(x_moe[...], s_a)
    send(ST_A, "gx", s_a, r_a, True)
    for c in loads[7:11] + loads[12:13]:
        c.wait()

    received(ST_D, r_d)
    everything = r_d[...].astype(F32).reshape(256, 128).astype(BF16)
    queries = mm(sel_e[...], everything)
    q_rows[...] = queries.reshape(32, 8, 128)
    queries = queries.astype(BF16)
    scores = []
    for g in range(KEY_VALUE_HEADS):
        kg = v_keys[:, :, pl.ds(128 * g, 128)].reshape(256, 128)
        scores.append(
            lax.dot_general(
                queries[32 * g : 32 * g + 32], kg, (((1,), (1,)), ((), ())), preferred_element_type=F32
            )
        )
    score = jnp.concatenate(scores, axis=0)
    weight = jnp.exp(CAP * jnp.tanh(score * (HEAD_SIZE**-0.5 / CAP))).reshape(32, 8, 256) * mask[...]
    weight = weight.reshape(256, 256)
    weight16 = weight.astype(BF16)
    sums = []
    for g in range(KEY_VALUE_HEADS):
        vg = v_vals[:, :, pl.ds(128 * g, 128)].reshape(256, 128)
        sums.append(mm(weight16[32 * g : 32 * g + 32], vg))
    summed = jnp.concatenate(sums, axis=0)
    total1 = jnp.broadcast_to(jnp.sum(weight, axis=1, keepdims=True), (256, 128))
    total0 = pltpu.roll(total1, 4, 0)
    row, lane = iota((256, 128), 0), iota((256, 128), 1)
    low1 = total1 - total1.astype(BF16).astype(F32)
    low0 = total0 - total0.astype(BF16).astype(F32)
    free = pick((lane & 63) >> 4, [total1, low1, total0, low0])
    keep = (((row >> 2) & 1) == 0) | ((lane >> 6) == ((row >> 3) & 1))
    s_e[...] = jnp.where(keep, summed, free).reshape(32, 8, 128).astype(BF16)
    send(ST_E, "gy", s_e, r_e, True)

    group = lax.div(gy, 4)
    second = lax.rem(group, 2)

    def fresh(first_block):
        tile = r_d[first_block + lax.div(group, 2)].astype(F32)
        return jnp.where((s8 >> 2) == second, tile, pltpu.roll(tile, 4, 0))

    own_query = q_rows[gy].astype(BF16).astype(F32)
    own_score = jnp.sum(own_query * fresh(24), axis=1, keepdims=True) * (HEAD_SIZE**-0.5 / CAP)
    own_weight = jnp.exp(CAP * jnp.tanh(own_score))
    own_value = own_weight.astype(BF16).astype(F32) * fresh(28)
    total_a = None

    received(ST_E, r_e)
    tile = total(r_e)
    half = (l8 >> 6) == core
    quarter = (l8 & 63) >> 5
    den1 = jnp.sum(jnp.where(~half & (quarter == 0), tile, 0.0), axis=1, keepdims=True) * 0.0625
    den0 = jnp.sum(jnp.where(~half & (quarter == 1), tile, 0.0), axis=1, keepdims=True) * 0.0625
    den1, den0 = jnp.broadcast_to(den1, (8, 128)), jnp.broadcast_to(den0, (8, 128))
    den = jnp.where(s8 < 4, pltpu.roll(den0, 4, 0), den1) + own_weight
    attended = (tile + own_value) / den
    t_f[...] = jnp.where((s8 < 4) | half, attended, 0.0).astype(BF16)
    send(ST_F, "gx", t_f, r_f, False)

    ctile = (iota((256, 128), 0) & 7) >> 1
    received(ST_F, r_f)
    rows = mm(sel_g[...], r_f[...].astype(F32).reshape(128, 128).astype(BF16))
    left = jnp.concatenate([rows[0:256], rows[256:512]], axis=1).astype(BF16)
    sums = mm(left, v_wo[...])
    s_g[...] = pick(ctile, [sums[:, 128 * c : 128 * c + 128] for c in range(3)]).reshape(32, 8, 128).astype(BF16)
    send(ST_G, "gy", s_g, r_g, True)
    received(ST_A, r_a)
    total_a = total(r_a)

    received(ST_G, r_g)
    branch = jnp.where(s8 < 6, total(r_g), 0.0)
    gained = branch * pg
    branch_t[...] = gained
    branch_sums = lane_sums(
        [(0, branch * branch), (1, base_t[...] * gained), (2, gained * gained)]
        + [(3 + e, gained * rm[e]) for e in range(8)]
    )
    t_j[...] = jnp.where(s8 < 6, gained * mg, split_terms(branch_sums)).astype(BF16)
    send(ST_J, "gy", t_j, r_j, False)

    received(ST_J, r_j)
    gate_up(r_j[...].astype(F32).reshape(256, 128).astype(BF16), s_k)
    send(ST_K, "gx", s_k, r_k, True)
    received(ST_K, r_k)
    total_k = total(r_k)

    sums_a, sums_k = join_terms(total_a[32:40]), join_terms(total_k[32:40])
    post = lax.rsqrt(sums_k[:, 0:1] / MODEL_WIDTH + EPS)
    stream_square = sums_a[:, 0:1] + 2.0 * post * sums_k[:, 1:2] + post * post * sums_k[:, 2:3]
    pre = lax.rsqrt(stream_square / MODEL_WIDTH + EPS)
    logits = pre * (sums_a + post * sums_k)
    named = (l8 >= 3) & (l8 < 11)
    exponent = jnp.where(named, jnp.exp(jnp.where(named, logits, 0.0)), 0.0)
    chance = exponent / jnp.sum(exponent, axis=1, keepdims=True)
    combine = jnp.sum(jnp.where(l8 == 3 + (s8 >> 1), chance, 0.0), axis=1, keepdims=True)
    combine = combine.astype(BF16).astype(F32)

    def spread(column, first):
        two = [jnp.broadcast_to(column[first + k : first + k + 1], (8, 128)) for k in range(2)]
        return jnp.where((s8 & 1) == 0, two[0], two[1])

    hidden = []
    for e in range(EXP_WIN):
        post_e, pre_e = spread(post, 2 * e), spread(pre, 2 * e)
        gate, up = (
            pre_e * (total_a[16 * e + 8 * u : 16 * e + 8 * u + 8] + post_e * total_k[16 * e + 8 * u : 16 * e + 8 * u + 8])
            for u in range(2)
        )
        bent = 0.5 * gate * (1.0 + jnp.tanh(math.sqrt(2.0 / math.pi) * (gate + 0.044715 * gate * gate * gate)))
        hidden.append(bent * up * spread(combine, 2 * e))
    t_h[...] = jnp.concatenate(hidden, axis=0).astype(BF16)
    send(ST_H, "gx", t_h, r_h, False)

    mixed_ref[...] = as_rows(base_t[...] + spread(post, 4) * branch_t[...]).astype(BF16)

    received(ST_H, r_h)
    hidden = r_h[...].astype(F32).reshape(256, 128).astype(BF16)
    sums = jnp.zeros((256, 384), F32)
    for e in range(EXP_WIN):
        rows = mm(perm_l[pl.ds(1024 * e, 1024)], hidden).astype(BF16)
        left = jnp.concatenate([rows[256 * ct : 256 * ct + 256] for ct in range(4)], axis=1)
        sums = sums + mm(left, v_wd[e])
    s_l[...] = pick(ctile, [sums[:, 128 * c : 128 * c + 128] for c in range(3)]).reshape(32, 8, 128).astype(BF16)
    send(ST_L, "gy", s_l, r_l, True)
    received(ST_L, r_l)
    out_ref[...] = as_rows(total(r_l)).astype(BF16)

    for stage, dst in (
        (ST_B, r_b), (ST_C, r_c), (ST_D, r_d), (ST_E, r_e), (ST_F, r_f), (ST_G, r_g), (ST_J, r_j), (ST_A, r_a),
        (ST_K, r_k), (ST_H, r_h), (ST_L, r_l),
    ):
        pltpu.make_async_copy(peers_of(dst), peers_of(dst), send_sem.at[stage]).wait()


def local(
    residual, attn_gain, wqkv, rotated_key_cache, slot_value_cache, lengths, starts, wo, post_gain, moe_gain, router,
    expert_ids, w_gate_up, w_down,
):
    anywhere = pl.BlockSpec(memory_space=pl.ANY)
    scalars = pl.BlockSpec(memory_space=pltpu.SMEM)
    vmem = pltpu.VMEM
    gy_tiles = vmem((NY, 8, 128), BF16)
    gx_tiles = vmem((NX, 8, 128), BF16)
    tile = vmem((8, 128), BF16)
    return pl.pallas_call(
        kernel,
        out_shape=(jax.ShapeDtypeStruct((2, 384), BF16), jax.ShapeDtypeStruct((2, 384), BF16)),
        in_specs=[anywhere] * 5 + [scalars] * 2 + [anywhere] * 7,
        out_specs=(pl.BlockSpec(memory_space=pltpu.VMEM), pl.BlockSpec(memory_space=pltpu.VMEM)),
        scratch_shapes=[
            vmem((2, 384), BF16), vmem((1, 384), F32), vmem((1, 384), F32), vmem((1, 384), F32), vmem((8, 384), BF16),
            vmem((2, 64), I32), vmem((384, 256), BF16), vmem((4, 64, 1024), BF16), vmem((4, 64, 1024), BF16),
            vmem((256, 384), BF16), vmem((2, 384, 2, 512), BF16), vmem((2, 512, 384), BF16),
            vmem((2, 2, 384, 512), BF16),
            vmem((512, 256), BF16), vmem((256, 256), BF16), vmem((512, 128), BF16), vmem((896, 256), BF16),
            vmem((2048, 256), BF16), vmem((8, 8, 128), F32), vmem((8, 256), F32), vmem((8, 128), F32),
            vmem((8, 128), F32), vmem((32, 8, 128), F32), vmem((256, 128), BF16),
            tile, gy_tiles, vmem((NX, 16, 128), BF16), vmem((NX, 16, 128), BF16), tile, gy_tiles, gy_tiles, gy_tiles,
            tile, gx_tiles, gy_tiles, gy_tiles, tile, gy_tiles, vmem((NX, 48, 128), BF16), vmem((NX, 48, 128), BF16),
            vmem((NX, 48, 128), BF16), vmem((NX, 48, 128), BF16), vmem((16, 128), BF16), vmem((NX, 16, 128), BF16),
            gy_tiles, gy_tiles,
            pltpu.SemaphoreType.DMA((13,)), pltpu.SemaphoreType.DMA((11,)), pltpu.SemaphoreType.DMA((11,)),
        ],
        compiler_params=pltpu.CompilerParams(
            collective_id=0, has_side_effects=True, vmem_limit_bytes=48 * 1024 * 1024
        ),
        name="decode_step",
    )(
        residual, attn_gain.reshape(1, 384), wqkv, rotated_key_cache, slot_value_cache, lengths, starts, wo,
        post_gain.reshape(1, 384), moe_gain.reshape(1, 384), router.T, expert_ids.T, w_gate_up, w_down,
    )


def solution(mesh):
    return jax.shard_map(
        local,
        mesh=mesh,
        in_specs=(
            P("gy", "gx"), P("gx"), P("gx", "gy"), P("gx", "gy", None), P("gx", "gy", None), P("gx"), P("gx"),
            P("gy", "gx"), P("gx"), P("gx"), P("gx", None), P(), P(None, "gx", None, "gy"), P(None, "gy", "gx"),
        ),
        out_specs=(P("gy", "gx"), P("gy", "gx")),
        check_vma=False,
    )
```

```python
import functools
import math

import jax
import jax.numpy as jnp
from jax import lax
from jax.experimental import pallas as pl
from jax.experimental.pallas import tpu as pltpu
from jax.sharding import PartitionSpec as P

MODEL_WIDTH = 6144
QUERY_HEADS = 48
KEY_VALUE_HEADS = 8
HEAD_SIZE = 128
WINDOW_SLOTS = 2048
EXP_WIN = 2
NX, NY = 16, 32
EPS = 1e-05
CAP = 30.0
F32, BF16, I32 = jnp.float32, jnp.bfloat16, jnp.int32
MESH = pl.DeviceIdType.MESH

ST_B, ST_C, ST_D, ST_E, ST_F, ST_G, ST_J, ST_A, ST_K, ST_H, ST_L = range(11)


def iota(shape, dim):
    return lax.broadcasted_iota(I32, shape, dim)


def onehot(condition):
    return jnp.where(condition, 1.0, 0.0).astype(BF16)


def mm(a, b):
    return jnp.dot(a, b, preferred_element_type=F32)


def pick(number, values):
    result = values[-1]
    for k in range(len(values) - 2, -1, -1):
        result = jnp.where(number == k, values[k], result)
    return result


def gain_tile(gain):
    s = iota((8, 128), 0)
    parts = [jnp.broadcast_to(gain[pl.ds(128 * c, 128)].reshape(1, 128), (8, 128)) for c in range(3)]
    return pick(s >> 1, parts + [jnp.ones((8, 128), F32)])


def fold_requests(v):
    u = v + pltpu.roll(v, 4, 0)
    return u + pltpu.roll(u, 2, 0)


def split_terms(v):
    hi = v.astype(BF16).astype(F32)
    rest = v - hi
    mid = rest.astype(BF16).astype(F32)
    low = rest - mid
    return hi + pltpu.roll(mid, 16, 1) + pltpu.roll(low, 32, 1)


def join_terms(v):
    return v + pltpu.roll(v, 112, 1) + pltpu.roll(v, 96, 1)


def as_rows(tile):
    return jnp.concatenate([tile[0:2], tile[2:4], tile[4:6]], axis=1)


def kernel(
    residual, attn_gain, wqkv, keys, values, lengths, starts, wo, post_gain, moe_gain, router, ids, w_gate_up, w_down,
    res_ref,
    v_res, v_ag, v_pg, v_mg, v_rt, v_ids, v_wqkv, v_keys, v_vals, v_wo, v_gu, v_wd, w_split,
    perm_c, sel_e, sel_g, perm_k, perm_l, rm, mask, base_t, branch_t, q_rows, x_moe,
    t_b, r_b, s_c, r_c, t_d, r_d, s_e, r_e, t_f, r_f, s_g, r_g, t_j, r_j, s_a, r_a, s_k, r_k, t_h, r_h, s_l, r_l,
    load_sem, send_sem, recv_sem,
):
    gx = lax.axis_index("gx")
    gy = lax.axis_index("gy")
    z, core = lax.div(gy, 2), lax.rem(gy, 2)
    px, py = lax.div(gx, 4), lax.rem(gx, 4)

    def over_gy(act):
        def body(q, carry):
            h = lax.div(q + 1, 2)
            far = lax.rem(z + 8 + h * (1 - 2 * lax.rem(q, 2)), 16)
            act(2 * far + core)
            act(2 * far + 1 - core)
            return carry

        lax.fori_loop(0, 15, body, 0)
        act(2 * z + 1 - core)

    def over_gx(act):
        def shift(t):
            return lax.rem(10 - lax.div(t * (t + 1), 2), 4)

        def body(k, carry):
            qx = lax.rem(px + shift(lax.div(k, 4)), 4)
            qy = lax.rem(py + shift(lax.rem(k, 4)), 4)
            act(4 * qx + qy)
            return carry

        lax.fori_loop(0, 15, body, 0)

    barrier = pltpu.get_barrier_semaphore()
    over_gy(lambda p: pl.semaphore_signal(barrier, inc=1, device_id=(gx, p), device_id_type=MESH))
    over_gx(lambda p: pl.semaphore_signal(barrier, inc=1, device_id=(p, gy), device_id_type=MESH))

    loads = []

    def load(src, dst, k):
        c = pltpu.make_async_copy(src, dst, load_sem.at[k])
        c.start()
        loads.append(c)

    load(residual, v_res, 0)
    load(attn_gain, v_ag, 1)
    load(post_gain, v_pg, 2)
    load(moe_gain, v_mg, 3)
    load(router, v_rt, 4)
    load(ids, v_ids, 5)
    load(wqkv, v_wqkv, 6)
    load(keys, v_keys, 7)
    load(values, v_vals, 8)
    load(wo.at[pl.ds(pl.multiple_of(64 * core, 64), 128)], v_wo.at[pl.ds(0, 128)], 9)
    load(
        wo.at[pl.ds(pl.multiple_of(128 * (1 - core), 64), 64)],
        v_wo.at[pl.ds(pl.multiple_of(128 + 64 * core, 64), 64)],
        10,
    )
    load(w_gate_up, v_gu, 11)
    load(w_down, v_wd, 12)

    def send(stage, along, src, dst, each):
        me = gy if along == "gy" else gx

        def act(p):
            pltpu.make_async_remote_copy(
                src_ref=src.at[p] if each else src,
                dst_ref=dst.at[me],
                send_sem=send_sem.at[stage],
                recv_sem=recv_sem.at[stage],
                device_id=(gx, p) if along == "gy" else (p, gy),
                device_id_type=MESH,
            ).start()

        (over_gy if along == "gy" else over_gx)(act)
        dst[me] = src[me] if each else src[...]

    def peers_of(dst):
        return dst.at[pl.ds(0, dst.shape[0] - 1)]

    def received(stage, dst):
        pltpu.make_async_copy(peers_of(dst), peers_of(dst), recv_sem.at[stage]).wait()

    def total(ref):
        return jnp.sum(ref[...].astype(F32), axis=0)

    s8, l8 = iota((8, 128), 0), iota((8, 128), 1)
    for c in loads[:6]:
        c.wait()
    res = v_res[...].astype(F32)
    base = jnp.concatenate([res[:, 0:128], res[:, 128:256], res[:, 256:384], jnp.zeros((2, 128), F32)], axis=0)
    base_t[...] = base
    ag, pg, mg = gain_tile(v_ag), gain_tile(v_pg), gain_tile(v_mg)
    rt = v_rt[...].astype(F32)
    for e in range(8):
        row = rt[e : e + 1]
        parts = [jnp.broadcast_to(row[:, 128 * c : 128 * c + 128], (8, 128)) for c in range(3)]
        rm[e] = pick(s8 >> 1, parts + [jnp.zeros((8, 128), F32)]) * mg

    def lane_sums(terms):
        acc = jnp.zeros((8, 128), F32)
        for k, term in terms:
            acc = jnp.where(l8 == k, jnp.sum(term, axis=1, keepdims=True), acc)
        return fold_requests(acc)

    base_sums = lane_sums([(0, base * base)] + [(3 + e, base * rm[e]) for e in range(8)])
    t_b[...] = jnp.where(s8 < 6, base, split_terms(base_sums)).astype(BF16)

    row, lane = iota((512, 256), 0), iota((512, 256), 1)
    n = 4 * ((row >> 3) & 15) + (row & 3)
    perm_c[...] = onehot(lane == ((n >> 1) << 3) + 2 * (row >> 7) + (n & 1))

    pl.semaphore_wait(barrier, NX + NY - 2)
    send(ST_B, "gy", t_b, r_b, False)

    row, lane = iota((256, 256), 0), iota((256, 256), 1)
    j, t = row >> 3, (row >> 2) & 1
    head = 3 * (j >> 1) + jnp.where(t == 1, 1, 2 * (j & 1))
    sel_e[...] = onehot(lane == ((head >> 1) << 3) + ((head & 1) << 2) + (row & 3))

    row, lane = iota((512, 128), 0), iota((512, 128), 1)
    s = row & 7
    n = 2 * ((row >> 3) & 31) + (s & 1)
    sel_g[...] = onehot((lane == ((n >> 2) << 3) + ((row >> 8) << 2) + (n & 3)) & (s < 6))

    lane_code, row_code = [], []
    id_rows = v_ids[...]
    for e in range(EXP_WIN):
        picked = jnp.where((id_rows[0:1] == e) | (id_rows[1:2] == e), 1.0, 0.0)
        a, b = iota((64, 64), 0), iota((64, 64), 1)
        column = jnp.sum(jnp.where(a == b, picked, 0.0), axis=1, keepdims=True)
        a, b = iota((64, 256), 0), iota((64, 256), 1)
        of = 2 * (b >> 3) + (b & 1)
        before = jnp.sum(jnp.where(a < of, column, 0.0), axis=0, keepdims=True)
        named = jnp.sum(jnp.where(a == of, column, 0.0), axis=0, keepdims=True)
        lane_code.append(jnp.where(named > 0.5, before, -1.0))
        a, b = iota((256, 64), 0), iota((256, 64), 1)
        of = 2 * (a >> 3) + (a & 1)
        before = jnp.sum(jnp.where(b < of, picked, 0.0), axis=1, keepdims=True)
        named = jnp.sum(jnp.where(b == of, picked, 0.0), axis=1, keepdims=True)
        row_code.append(jnp.where(named > 0.5, before, -1.0))

    row, lane = iota((128, 256), 0), iota((128, 256), 1)
    q, s = row & 7, lane & 7
    slot = (2 * (row >> 3) + (row & 1)).astype(F32)
    for e in range(EXP_WIN):
        here = slot == lane_code[e]
        for c in range(3):
            perm_k[pl.ds((3 * e + c) * 128, 128)] = onehot(here & ((s >> 1) == c))
    sums_here = (
        ((q >> 1) == 0) & (slot == lane_code[0]) | ((q >> 1) == 1) & (slot == lane_code[1])
    ) & ((s >> 1) == 3)
    own = ((q >> 1) == 2) & (lane == 8 * gy + 6 + (q & 1))
    perm_k[pl.ds(768, 128)] = onehot(sums_here | own)

    row, lane = iota((256, 256), 0), iota((256, 256), 1)
    slot = (2 * (lane >> 4) + (lane & 1)).astype(F32)
    for e in range(EXP_WIN):
        here = (slot == row_code[e]) & (((lane >> 3) & 1) == e) & ((row & 7) < 6)
        for ct in range(4):
            perm_l[pl.ds((4 * e + ct) * 256, 256)] = onehot(here & (((lane >> 1) & 3) == ct))

    row, lane = iota((8, 256), 0), iota((8, 256), 1)
    last = pick(lane >> 6, [lengths[r] for r in range(4)]) - 1
    first = pick(lane >> 6, [starts[r] for r in range(4)])
    position = last - ((last - (64 * gy + (lane & 63))) & (WINDOW_SLOTS - 1))
    usable = (position >= jnp.maximum(first, last - (WINDOW_SLOTS - 2))) & ((lane >> 6) == (row & 3))
    mask[...] = jnp.where(usable, 1.0, 0.0)

    turn = (l8 & 63).astype(F32)
    angle = pick(s8 & 3, [lengths[r] for r in range(4)]).astype(F32) * jnp.exp(turn * (-2.0 * math.log(10000.0) / 128))
    rotated = 2 * gy < QUERY_HEADS + KEY_VALUE_HEADS
    cosine = jnp.where(rotated, jnp.cos(angle), 1.0)
    sine = jnp.where(rotated, jnp.where(l8 < 64, -1.0, 1.0) * jnp.sin(angle), 0.0)

    v_wo[pl.ds(pl.multiple_of(192 - 64 * core, 64), 64)] = jnp.zeros((64, 384), BF16)
    loads[6].wait()

    received(ST_B, r_b)
    x = r_b[...].astype(F32)
    rows = mm(perm_c[...], (x * ag).reshape(256, 128).astype(BF16))
    left = jnp.concatenate([rows[128 * c : 128 * c + 128] for c in range(3)], axis=1).astype(BF16)
    sums = mm(left, v_wqkv[...])
    hh = (iota((128, 128), 0) >> 2) & 1
    sums = jnp.where(hh == 0, sums[:, 0:128], sums[:, 128:256])
    s_c[...] = jnp.concatenate([sums.reshape(16, 8, 128), rows[384:512].reshape(16, 8, 128)], axis=1).astype(BF16)
    send(ST_C, "gx", s_c, r_c, True)
    x_moe[...] = (x * mg).reshape(256, 128).astype(BF16)
    for c in loads[11:12]:
        c.wait()
    for e in range(EXP_WIN):
        for u in range(2):
            w_split[e, u] = v_gu[e, :, u, :]

    received(ST_C, r_c)
    both = total(r_c)
    square = join_terms(both[8:16])
    scale = lax.rsqrt(square[:, 0:1] / MODEL_WIDTH + EPS)
    heads = both[0:8] * scale
    heads = heads * cosine + pltpu.roll(heads, 64, 1) * sine
    t_d[...] = heads.astype(BF16)
    send(ST_D, "gy", t_d, r_d, False)

    def gate_up(x_rows, out):
        rows = mm(perm_k[...], x_rows)
        rows16 = rows.astype(BF16)
        ct = (iota((128, 128), 0) & 7) >> 1
        for e in range(EXP_WIN):
            left = jnp.concatenate([rows16[(3 * e + c) * 128 : (3 * e + c) * 128 + 128] for c in range(3)], axis=1)
            halves = []
            for u in range(2):
                full = mm(left, w_split[e, u])
                halves.append(pick(ct, [full[:, 128 * k : 128 * k + 128] for k in range(4)]).reshape(16, 8, 128))
            out[:, pl.ds(16 * e, 16), :] = jnp.concatenate(halves, axis=1).astype(BF16)
        sums = rows[768:896].reshape(16, 8, 128)
        out[:, pl.ds(32, 16), :] = jnp.concatenate([sums, jnp.zeros((16, 8, 128), F32)], axis=1).astype(BF16)

    gate_up(x_moe[...], s_a)
    send(ST_A, "gx", s_a, r_a, True)
    for c in loads[7:11] + loads[12:13]:
        c.wait()

    received(ST_D, r_d)
    everything = r_d[...].astype(F32).reshape(256, 128).astype(BF16)
    queries = mm(sel_e[...], everything)
    q_rows[...] = queries.reshape(32, 8, 128)
    queries = queries.astype(BF16)
    scores = []
    for g in range(KEY_VALUE_HEADS):
        kg = v_keys[:, :, pl.ds(128 * g, 128)].reshape(256, 128)
        scores.append(
            lax.dot_general(
                queries[32 * g : 32 * g + 32], kg, (((1,), (1,)), ((), ())), preferred_element_type=F32
            )
        )
    score = jnp.concatenate(scores, axis=0)
    weight = jnp.exp(CAP * jnp.tanh(score * (HEAD_SIZE**-0.5 / CAP))).reshape(32, 8, 256) * mask[...]
    weight = weight.reshape(256, 256)
    weight16 = weight.astype(BF16)
    sums = []
    for g in range(KEY_VALUE_HEADS):
        vg = v_vals[:, :, pl.ds(128 * g, 128)].reshape(256, 128)
        sums.append(mm(weight16[32 * g : 32 * g + 32], vg))
    summed = jnp.concatenate(sums, axis=0)
    total1 = jnp.broadcast_to(jnp.sum(weight, axis=1, keepdims=True), (256, 128))
    total0 = pltpu.roll(total1, 4, 0)
    row, lane = iota((256, 128), 0), iota((256, 128), 1)
    low1 = total1 - total1.astype(BF16).astype(F32)
    low0 = total0 - total0.astype(BF16).astype(F32)
    free = pick((lane & 63) >> 4, [total1, low1, total0, low0])
    keep = (((row >> 2) & 1) == 0) | ((lane >> 6) == ((row >> 3) & 1))
    s_e[...] = jnp.where(keep, summed, free).reshape(32, 8, 128).astype(BF16)
    send(ST_E, "gy", s_e, r_e, True)

    group = lax.div(gy, 4)
    second = lax.rem(group, 2)

    def fresh(first_block):
        tile = r_d[first_block + lax.div(group, 2)].astype(F32)
        return jnp.where((s8 >> 2) == second, tile, pltpu.roll(tile, 4, 0))

    own_query = q_rows[gy].astype(BF16).astype(F32)
    own_score = jnp.sum(own_query * fresh(24), axis=1, keepdims=True) * (HEAD_SIZE**-0.5 / CAP)
    own_weight = jnp.exp(CAP * jnp.tanh(own_score))
    own_value = own_weight.astype(BF16).astype(F32) * fresh(28)
    total_a = None

    received(ST_E, r_e)
    tile = total(r_e)
    half = (l8 >> 6) == core
    quarter = (l8 & 63) >> 5
    den1 = jnp.sum(jnp.where(~half & (quarter == 0), tile, 0.0), axis=1, keepdims=True) * 0.0625
    den0 = jnp.sum(jnp.where(~half & (quarter == 1), tile, 0.0), axis=1, keepdims=True) * 0.0625
    den1, den0 = jnp.broadcast_to(den1, (8, 128)), jnp.broadcast_to(den0, (8, 128))
    den = jnp.where(s8 < 4, pltpu.roll(den0, 4, 0), den1) + own_weight
    attended = (tile + own_value) / den
    t_f[...] = jnp.where((s8 < 4) | half, attended, 0.0).astype(BF16)
    send(ST_F, "gx", t_f, r_f, False)

    ctile = (iota((256, 128), 0) & 7) >> 1
    received(ST_F, r_f)
    rows = mm(sel_g[...], r_f[...].astype(F32).reshape(128, 128).astype(BF16))
    left = jnp.concatenate([rows[0:256], rows[256:512]], axis=1).astype(BF16)
    sums = mm(left, v_wo[...])
    s_g[...] = pick(ctile, [sums[:, 128 * c : 128 * c + 128] for c in range(3)]).reshape(32, 8, 128).astype(BF16)
    send(ST_G, "gy", s_g, r_g, True)
    received(ST_A, r_a)
    total_a = total(r_a)

    received(ST_G, r_g)
    branch = jnp.where(s8 < 6, total(r_g), 0.0)
    gained = branch * pg
    branch_t[...] = gained
    branch_sums = lane_sums(
        [(0, branch * branch), (1, base_t[...] * gained), (2, gained * gained)]
        + [(3 + e, gained * rm[e]) for e in range(8)]
    )
    t_j[...] = jnp.where(s8 < 6, gained * mg, split_terms(branch_sums)).astype(BF16)
    send(ST_J, "gy", t_j, r_j, False)

    received(ST_J, r_j)
    gate_up(r_j[...].astype(F32).reshape(256, 128).astype(BF16), s_k)
    send(ST_K, "gx", s_k, r_k, True)
    received(ST_K, r_k)
    total_k = total(r_k)

    sums_a, sums_k = join_terms(total_a[32:40]), join_terms(total_k[32:40])
    post = lax.rsqrt(sums_k[:, 0:1] / MODEL_WIDTH + EPS)
    stream_square = sums_a[:, 0:1] + 2.0 * post * sums_k[:, 1:2] + post * post * sums_k[:, 2:3]
    pre = lax.rsqrt(stream_square / MODEL_WIDTH + EPS)
    logits = pre * (sums_a + post * sums_k)
    named = (l8 >= 3) & (l8 < 11)
    exponent = jnp.where(named, jnp.exp(jnp.where(named, logits, 0.0)), 0.0)
    chance = exponent / jnp.sum(exponent, axis=1, keepdims=True)
    combine = jnp.sum(jnp.where(l8 == 3 + (s8 >> 1), chance, 0.0), axis=1, keepdims=True)
    combine = combine.astype(BF16).astype(F32)

    def spread(column, first):
        two = [jnp.broadcast_to(column[first + k : first + k + 1], (8, 128)) for k in range(2)]
        return jnp.where((s8 & 1) == 0, two[0], two[1])

    hidden = []
    for e in range(EXP_WIN):
        post_e, pre_e = spread(post, 2 * e), spread(pre, 2 * e)
        gate, up = (
            pre_e * (total_a[16 * e + 8 * u : 16 * e + 8 * u + 8] + post_e * total_k[16 * e + 8 * u : 16 * e + 8 * u + 8])
            for u in range(2)
        )
        bent = 0.5 * gate * (1.0 + jnp.tanh(math.sqrt(2.0 / math.pi) * (gate + 0.044715 * gate * gate * gate)))
        hidden.append(bent * up * spread(combine, 2 * e))
    t_h[...] = jnp.concatenate(hidden, axis=0).astype(BF16)
    send(ST_H, "gx", t_h, r_h, False)

    mixed = as_rows(base_t[...] + spread(post, 4) * branch_t[...])

    received(ST_H, r_h)
    hidden = r_h[...].astype(F32).reshape(256, 128).astype(BF16)
    sums = jnp.zeros((256, 384), F32)
    for e in range(EXP_WIN):
        rows = mm(perm_l[pl.ds(1024 * e, 1024)], hidden).astype(BF16)
        left = jnp.concatenate([rows[256 * ct : 256 * ct + 256] for ct in range(4)], axis=1)
        sums = sums + mm(left, v_wd[e])
    s_l[...] = pick(ctile, [sums[:, 128 * c : 128 * c + 128] for c in range(3)]).reshape(32, 8, 128).astype(BF16)
    send(ST_L, "gy", s_l, r_l, True)
    received(ST_L, r_l)
    res_ref[...] = jnp.concatenate([mixed, as_rows(total(r_l))], axis=0).astype(BF16)

    for stage, dst in (
        (ST_B, r_b), (ST_C, r_c), (ST_D, r_d), (ST_E, r_e), (ST_F, r_f), (ST_G, r_g), (ST_J, r_j), (ST_A, r_a),
        (ST_K, r_k), (ST_H, r_h), (ST_L, r_l),
    ):
        pltpu.make_async_copy(peers_of(dst), peers_of(dst), send_sem.at[stage]).wait()


def local(
    residual, attn_gain, wqkv, rotated_key_cache, slot_value_cache, lengths, starts, wo, post_gain, moe_gain, router,
    expert_ids, w_gate_up, w_down,
):
    anywhere = pl.BlockSpec(memory_space=pltpu.HBM)
    scalars = pl.BlockSpec(memory_space=pltpu.SMEM)
    vmem = pltpu.VMEM
    gy_tiles = vmem((NY, 8, 128), BF16)
    gx_tiles = vmem((NX, 8, 128), BF16)
    tile = vmem((8, 128), BF16)
    result = pl.pallas_call(
        kernel,
        out_shape=jax.ShapeDtypeStruct((4, 384), BF16),
        in_specs=[anywhere] * 5 + [scalars] * 2 + [anywhere] * 7,
        out_specs=pl.BlockSpec(memory_space=pltpu.VMEM),
        scratch_shapes=[
            vmem((2, 384), BF16), vmem((384,), F32), vmem((384,), F32), vmem((384,), F32), vmem((8, 384), BF16),
            vmem((2, 64), I32), vmem((384, 256), BF16), vmem((4, 64, 1024), BF16), vmem((4, 64, 1024), BF16),
            vmem((256, 384), BF16), vmem((2, 384, 2, 512), BF16), vmem((2, 512, 384), BF16),
            vmem((2, 2, 384, 512), BF16),
            vmem((512, 256), BF16), vmem((256, 256), BF16), vmem((512, 128), BF16), vmem((896, 256), BF16),
            vmem((2048, 256), BF16), vmem((8, 8, 128), F32), vmem((8, 256), F32), vmem((8, 128), F32),
            vmem((8, 128), F32), vmem((32, 8, 128), F32), vmem((256, 128), BF16),
            tile, gy_tiles, vmem((NX, 16, 128), BF16), vmem((NX, 16, 128), BF16), tile, gy_tiles, gy_tiles, gy_tiles,
            tile, gx_tiles, gy_tiles, gy_tiles, tile, gy_tiles, vmem((NX, 48, 128), BF16), vmem((NX, 48, 128), BF16),
            vmem((NX, 48, 128), BF16), vmem((NX, 48, 128), BF16), vmem((16, 128), BF16), vmem((NX, 16, 128), BF16),
            gy_tiles, gy_tiles,
            pltpu.SemaphoreType.DMA((13,)), pltpu.SemaphoreType.DMA((11,)), pltpu.SemaphoreType.DMA((11,)),
        ],
        compiler_params=pltpu.CompilerParams(
            collective_id=0, has_side_effects=True, vmem_limit_bytes=63 * 1024 * 1024
        ),
        name="decode_step",
    )(
        residual, attn_gain, wqkv, rotated_key_cache, slot_value_cache, lengths, starts, wo,
        post_gain, moe_gain, router.T, expert_ids.T, w_gate_up, w_down,
    )
    return result[:2], result[2:]


def solution(mesh):
    return jax.shard_map(
        local,
        mesh=mesh,
        in_specs=(
            P("gy", "gx"), P("gx"), P("gx", "gy"), P("gx", "gy", None), P("gx", "gy", None), P("gx"), P("gx"),
            P("gy", "gx"), P("gx"), P("gx"), P("gx", None), P(), P(None, "gx", None, "gy"), P(None, "gy", "gx"),
        ),
        out_specs=(P("gy", "gx"), P("gy", "gx")),
        check_vma=False,
    )
```

```python
import functools
import math

import jax
import jax.numpy as jnp
from jax import lax
from jax.experimental import pallas as pl
from jax.experimental.pallas import tpu as pltpu
from jax.sharding import PartitionSpec as P

MODEL_WIDTH = 6144
QUERY_HEADS = 48
KEY_VALUE_HEADS = 8
HEAD_SIZE = 128
WINDOW_SLOTS = 2048
EXP_WIN = 2
NX, NY = 16, 32
EPS = 1e-05
CAP = 30.0
F32, BF16, I32 = jnp.float32, jnp.bfloat16, jnp.int32
MESH = pl.DeviceIdType.MESH

ST_B, ST_C, ST_D, ST_E, ST_F, ST_G, ST_J, ST_A, ST_K, ST_H, ST_L, ST_X = range(12)


def iota(shape, dim):
    return lax.broadcasted_iota(I32, shape, dim)


def onehot(condition):
    return jnp.where(condition, 1.0, 0.0).astype(BF16)


def mm(a, b):
    return jnp.dot(a, b, preferred_element_type=F32)


def pick(number, values):
    result = values[-1]
    for k in range(len(values) - 2, -1, -1):
        result = jnp.where(number == k, values[k], result)
    return result


def gain_tile(gain):
    s = iota((8, 128), 0)
    parts = [jnp.broadcast_to(gain[pl.ds(128 * c, 128)].reshape(1, 128), (8, 128)) for c in range(3)]
    return pick(s >> 1, parts + [jnp.ones((8, 128), F32)])


def fold_requests(v):
    u = v + pltpu.roll(v, 4, 0)
    return u + pltpu.roll(u, 2, 0)


def split_terms(v):
    hi = v.astype(BF16).astype(F32)
    rest = v - hi
    mid = rest.astype(BF16).astype(F32)
    low = rest - mid
    return hi + pltpu.roll(mid, 16, 1) + pltpu.roll(low, 32, 1)


def join_terms(v):
    return v + pltpu.roll(v, 112, 1) + pltpu.roll(v, 96, 1)


def place_of(n):
    return (((n >> 2) & 7) << 2) + (((n >> 1) & 1) << 1) + (n >> 5)


def request_at(index):
    return (((index >> 5) + (((index >> 3) & 1) << 3)) << 2) + (((index >> 4) & 1) << 1) + (index & 1)


def as_rows(tile):
    return jnp.concatenate([tile[0:2], tile[2:4], tile[4:6]], axis=1)


def kernel(
    residual, attn_gain, wqkv, keys, values, lengths, starts, wo, post_gain, moe_gain, router, ids, w_gate_up, w_down,
    res_ref,
    v_res, v_ag, v_pg, v_mg, v_rt, v_ids, v_wqkv, v_keys, v_vals, v_wo, v_gu, v_wd, w_split,
    perm_c, sel_e, sel_g, perm_k, perm_l, rm, mask, base_t, branch_t, q_rows, x_moe,
    t_b, r_b, s_c, r_c, t_d, r_d, s_e, r_e, t_f, r_f, s_x, r_x, s_g, r_g, t_j, r_j, s_a, r_a, s_k, r_k, t_h, r_h, s_l, r_l,
    load_sem, send_sem, recv_sem,
):
    gx = lax.axis_index("gx")
    gy = lax.axis_index("gy")
    z, core = lax.div(gy, 2), lax.rem(gy, 2)
    px, py = lax.div(gx, 4), lax.rem(gx, 4)
    low_z, high = lax.rem(z, 8), lax.div(z, 8)
    pair = 2 * low_z + core
    place = 2 * pair + high

    def over_gy(act):
        def body(q, carry):
            h = lax.div(q + 1, 2)
            far = lax.rem(z + 8 + h * (1 - 2 * lax.rem(q, 2)), 16)
            act(2 * far + core)
            act(2 * far + 1 - core)
            return carry

        lax.fori_loop(0, 15, body, 0)
        act(2 * z + 1 - core)

    def over_gx(act):
        def shift(t):
            return lax.rem(10 - lax.div(t * (t + 1), 2), 4)

        def body(k, carry):
            qx = lax.rem(px + shift(lax.div(k, 4)), 4)
            qy = lax.rem(py + shift(lax.rem(k, 4)), 4)
            act(4 * qx + qy)
            return carry

        lax.fori_loop(0, 15, body, 0)

    barrier = pltpu.get_barrier_semaphore()
    over_gy(lambda p: pl.semaphore_signal(barrier, inc=1, device_id=(gx, p), device_id_type=MESH))
    over_gx(lambda p: pl.semaphore_signal(barrier, inc=1, device_id=(p, gy), device_id_type=MESH))

    loads = []

    def load(src, dst, k):
        c = pltpu.make_async_copy(src, dst, load_sem.at[k])
        c.start()
        loads.append(c)

    load(residual, v_res, 0)
    load(attn_gain, v_ag, 1)
    load(post_gain, v_pg, 2)
    load(moe_gain, v_mg, 3)
    load(router, v_rt, 4)
    load(ids, v_ids, 5)
    load(wqkv, v_wqkv, 6)
    load(keys, v_keys, 7)
    load(values, v_vals, 8)
    load(wo.at[pl.ds(pl.multiple_of(64 * core, 64), 128)], v_wo.at[pl.ds(0, 128)], 9)
    load(
        wo.at[pl.ds(pl.multiple_of(128 * (1 - core), 64), 64)],
        v_wo.at[pl.ds(pl.multiple_of(128 + 64 * core, 64), 64)],
        10,
    )
    load(w_gate_up, v_gu, 11)
    load(w_down, v_wd, 12)

    def send(stage, along, src, dst, each):
        me = gy if along == "gy" else gx

        def act(p):
            pltpu.make_async_remote_copy(
                src_ref=src.at[p] if each else src,
                dst_ref=dst.at[me],
                send_sem=send_sem.at[stage],
                recv_sem=recv_sem.at[stage],
                device_id=(gx, p) if along == "gy" else (p, gy),
                device_id_type=MESH,
            ).start()

        (over_gy if along == "gy" else over_gx)(act)
        dst[me] = src[me] if each else src[...]

    def over_z(act):
        def body(q, carry):
            h = lax.div(q + 1, 2)
            act(lax.rem(z + 8 + h * (1 - 2 * lax.rem(q, 2)), 16))
            return carry

        lax.fori_loop(0, 15, body, 0)

    def over_near(act):
        def body(q, carry):
            h = lax.div(q + 1, 2)
            near = lax.rem(z + 16 + (4 - h) * (2 * lax.rem(q, 2) - 1), 16)
            act(2 * near + core)
            act(2 * near + 1 - core)
            return carry

        lax.fori_loop(0, 7, body, 0)
        act(2 * z + 1 - core)

    def push(stage, src, dst, p):
        pltpu.make_async_remote_copy(
            src_ref=src,
            dst_ref=dst,
            send_sem=send_sem.at[stage],
            recv_sem=recv_sem.at[stage],
            device_id=(gx, p),
            device_id_type=MESH,
        ).start()

    def peers_of(dst):
        return dst.at[pl.ds(0, dst.shape[0] - 1)]

    def received(stage, dst):
        pltpu.make_async_copy(peers_of(dst), peers_of(dst), recv_sem.at[stage]).wait()

    def total(ref):
        return jnp.sum(ref[...].astype(F32), axis=0)

    s8, l8 = iota((8, 128), 0), iota((8, 128), 1)
    for c in loads[:6]:
        c.wait()
    res = v_res[...].astype(F32)
    base = jnp.concatenate([res[:, 0:128], res[:, 128:256], res[:, 256:384], jnp.zeros((2, 128), F32)], axis=0)
    base_t[...] = base
    ag, pg, mg = gain_tile(v_ag), gain_tile(v_pg), gain_tile(v_mg)
    rt = v_rt[...].astype(F32)
    for e in range(8):
        row = rt[e : e + 1]
        parts = [jnp.broadcast_to(row[:, 128 * c : 128 * c + 128], (8, 128)) for c in range(3)]
        rm[e] = pick(s8 >> 1, parts + [jnp.zeros((8, 128), F32)]) * mg

    def lane_sums(terms):
        acc = jnp.zeros((8, 128), F32)
        for k, term in terms:
            acc = jnp.where(l8 == k, jnp.sum(term, axis=1, keepdims=True), acc)
        return fold_requests(acc)

    base_sums = lane_sums([(0, base * base)] + [(3 + e, base * rm[e]) for e in range(8)])
    t_b[...] = jnp.where(s8 < 6, base, split_terms(base_sums)).astype(BF16)

    row, lane = iota((512, 256), 0), iota((512, 256), 1)
    n = 4 * ((row >> 3) & 15) + (row & 3)
    perm_c[...] = onehot(lane == (place_of(n) << 3) + 2 * (row >> 7) + (n & 1))

    pl.semaphore_wait(barrier, NX + NY - 2)
    over_gy(lambda p: push(ST_B, t_b, r_b.at[place], p))
    r_b[place] = t_b[...]

    row, lane = iota((256, 256), 0), iota((256, 256), 1)
    j, t = row >> 3, (row >> 2) & 1
    head = 3 * (j >> 1) + jnp.where(t == 1, 1, 2 * (j & 1))
    sel_e[...] = onehot(lane == ((head >> 1) << 3) + ((head & 1) << 2) + (row & 3))

    row, lane = iota((512, 128), 0), iota((512, 128), 1)
    s = row & 7
    n = ((((row >> 4) & 7) + (((row >> 3) & 1) << 3)) << 2) + 2 * (core + (row >> 8) * (1 - 2 * core)) + (s & 1)
    sel_g[...] = onehot((lane == ((n >> 2) << 3) + (((row >> 7) & 1) << 2) + (n & 3)) & (s < 6))

    lane_code, row_code = [], []
    id_rows = v_ids[...]
    for e in range(EXP_WIN):
        picked = jnp.where((id_rows[0:1] == e) | (id_rows[1:2] == e), 1.0, 0.0)
        a, b = iota((64, 64), 0), iota((64, 64), 1)
        column = jnp.sum(jnp.where(a == b, picked, 0.0), axis=1, keepdims=True)
        a, b = iota((64, 256), 0), iota((64, 256), 1)
        of = request_at(b)
        before = jnp.sum(jnp.where(a < of, column, 0.0), axis=0, keepdims=True)
        named = jnp.sum(jnp.where(a == of, column, 0.0), axis=0, keepdims=True)
        lane_code.append(jnp.where(named > 0.5, before, -1.0))
        a, b = iota((256, 64), 0), iota((256, 64), 1)
        of = 2 * (a >> 3) + (a & 1)
        before = jnp.sum(jnp.where(b < of, picked, 0.0), axis=1, keepdims=True)
        named = jnp.sum(jnp.where(b == of, picked, 0.0), axis=1, keepdims=True)
        row_code.append(jnp.where(named > 0.5, before, -1.0))

    row, lane = iota((128, 256), 0), iota((128, 256), 1)
    q, s = row & 7, lane & 7
    slot = (2 * (row >> 3) + (row & 1)).astype(F32)
    for e in range(EXP_WIN):
        here = slot == lane_code[e]
        for c in range(3):
            perm_k[pl.ds((3 * e + c) * 128, 128)] = onehot(here & ((s >> 1) == c))
    sums_here = (
        ((q >> 1) == 0) & (slot == lane_code[0]) | ((q >> 1) == 1) & (slot == lane_code[1])
    ) & ((s >> 1) == 3)
    own = ((q >> 1) == 2) & (lane == 8 * place + 6 + (q & 1))
    perm_k[pl.ds(768, 128)] = onehot(sums_here | own)

    row, lane = iota((256, 256), 0), iota((256, 256), 1)
    slot = (2 * (lane >> 4) + (lane & 1)).astype(F32)
    for e in range(EXP_WIN):
        here = (slot == row_code[e]) & (((lane >> 3) & 1) == e) & ((row & 7) < 6)
        for ct in range(4):
            perm_l[pl.ds((4 * e + ct) * 256, 256)] = onehot(here & (((lane >> 1) & 3) == ct))

    row, lane = iota((8, 256), 0), iota((8, 256), 1)
    last = pick(lane >> 6, [lengths[r] for r in range(4)]) - 1
    first = pick(lane >> 6, [starts[r] for r in range(4)])
    position = last - ((last - (64 * gy + (lane & 63))) & (WINDOW_SLOTS - 1))
    usable = (position >= jnp.maximum(first, last - (WINDOW_SLOTS - 2))) & ((lane >> 6) == (row & 3))
    mask[...] = jnp.where(usable, 1.0, 0.0)

    turn = (l8 & 63).astype(F32)
    angle = pick(s8 & 3, [lengths[r] for r in range(4)]).astype(F32) * jnp.exp(turn * (-2.0 * math.log(10000.0) / 128))
    rotated = 2 * gy < QUERY_HEADS + KEY_VALUE_HEADS
    cosine = jnp.where(rotated, jnp.cos(angle), 1.0)
    sine = jnp.where(rotated, jnp.where(l8 < 64, -1.0, 1.0) * jnp.sin(angle), 0.0)

    v_wo[pl.ds(pl.multiple_of(192 - 64 * core, 64), 64)] = jnp.zeros((64, 384), BF16)
    loads[6].wait()

    received(ST_B, r_b)
    x = r_b[...].astype(F32)
    rows = mm(perm_c[...], (x * ag).reshape(256, 128).astype(BF16))
    left = jnp.concatenate([rows[128 * c : 128 * c + 128] for c in range(3)], axis=1).astype(BF16)
    sums = mm(left, v_wqkv[...])
    hh = (iota((128, 128), 0) >> 2) & 1
    sums = jnp.where(hh == 0, sums[:, 0:128], sums[:, 128:256])
    s_c[...] = jnp.concatenate([sums.reshape(16, 8, 128), rows[384:512].reshape(16, 8, 128)], axis=1)
    send(ST_C, "gx", s_c, r_c, True)
    x_moe[...] = (x * mg).reshape(256, 128).astype(BF16)
    for c in loads[11:12]:
        c.wait()
    for e in range(EXP_WIN):
        for u in range(2):
            w_split[e, u] = v_gu[e, :, u, :]

    received(ST_C, r_c)
    both = total(r_c)
    square = join_terms(both[8:16])
    scale = lax.rsqrt(square[:, 0:1] / MODEL_WIDTH + EPS)
    heads = both[0:8] * scale
    heads = heads * cosine + pltpu.roll(heads, 64, 1) * sine
    t_d[...] = heads.astype(BF16)
    send(ST_D, "gy", t_d, r_d, False)

    def gate_up(x_rows, out):
        rows = mm(perm_k[...], x_rows)
        rows16 = rows.astype(BF16)
        ct = (iota((128, 128), 0) & 7) >> 1
        for e in range(EXP_WIN):
            left = jnp.concatenate([rows16[(3 * e + c) * 128 : (3 * e + c) * 128 + 128] for c in range(3)], axis=1)
            halves = []
            for u in range(2):
                full = mm(left, w_split[e, u])
                halves.append(pick(ct, [full[:, 128 * k : 128 * k + 128] for k in range(4)]).reshape(16, 8, 128))
            out[:, pl.ds(16 * e, 16), :] = jnp.concatenate(halves, axis=1).astype(BF16)
        sums = rows[768:896].reshape(16, 8, 128)
        out[:, pl.ds(32, 8), :] = sums.astype(BF16)

    gate_up(x_moe[...], s_a)
    send(ST_A, "gx", s_a, r_a, True)
    for c in loads[7:11] + loads[12:13]:
        c.wait()

    received(ST_D, r_d)
    everything = r_d[...].astype(F32).reshape(256, 128).astype(BF16)
    queries = mm(sel_e[...], everything)
    q_rows[...] = queries.reshape(32, 8, 128)
    queries = queries.astype(BF16)
    scores = []
    for g in range(KEY_VALUE_HEADS):
        kg = v_keys[:, :, pl.ds(128 * g, 128)].reshape(256, 128)
        scores.append(
            lax.dot_general(
                queries[32 * g : 32 * g + 32], kg, (((1,), (1,)), ((), ())), preferred_element_type=F32
            )
        )
    score = jnp.concatenate(scores, axis=0)
    weight = jnp.exp(CAP * jnp.tanh(score * (HEAD_SIZE**-0.5 / CAP))).reshape(32, 8, 256) * mask[...]
    weight = weight.reshape(256, 256)
    weight16 = weight.astype(BF16)
    sums = []
    for g in range(KEY_VALUE_HEADS):
        vg = v_vals[:, :, pl.ds(128 * g, 128)].reshape(256, 128)
        sums.append(mm(weight16[32 * g : 32 * g + 32], vg))
    summed = jnp.concatenate(sums, axis=0)
    total1 = jnp.broadcast_to(jnp.sum(weight, axis=1, keepdims=True), (256, 128))
    total0 = pltpu.roll(total1, 4, 0)
    row, lane = iota((256, 128), 0), iota((256, 128), 1)
    low1 = total1 - total1.astype(BF16).astype(F32)
    low0 = total0 - total0.astype(BF16).astype(F32)
    free = pick((lane & 63) >> 4, [total1, low1, total0, low0])
    keep = (((row >> 2) & 1) == 0) | ((lane >> 6) == ((row >> 3) & 1))
    s_e[...] = jnp.where(keep, summed, free).reshape(32, 8, 128).astype(BF16)
    send(ST_E, "gy", s_e, r_e, True)

    group = lax.div(gy, 4)
    second = lax.rem(group, 2)

    def fresh(first_block):
        tile = r_d[first_block + lax.div(group, 2)].astype(F32)
        return jnp.where((s8 >> 2) == second, tile, pltpu.roll(tile, 4, 0))

    own_query = q_rows[gy].astype(BF16).astype(F32)
    own_score = jnp.sum(own_query * fresh(24), axis=1, keepdims=True) * (HEAD_SIZE**-0.5 / CAP)
    own_weight = jnp.exp(CAP * jnp.tanh(own_score))
    own_value = own_weight.astype(BF16).astype(F32) * fresh(28)

    received(ST_E, r_e)
    tile = total(r_e)
    half = (l8 >> 6) == core
    quarter = (l8 & 63) >> 5
    den1 = jnp.sum(jnp.where(~half & (quarter == 0), tile, 0.0), axis=1, keepdims=True) * 0.0625
    den0 = jnp.sum(jnp.where(~half & (quarter == 1), tile, 0.0), axis=1, keepdims=True) * 0.0625
    den1, den0 = jnp.broadcast_to(den1, (8, 128)), jnp.broadcast_to(den0, (8, 128))
    den = jnp.where(s8 < 4, pltpu.roll(den0, 4, 0), den1) + own_weight
    attended = (tile + own_value) / den
    t_f[...] = jnp.where((s8 < 4) | half, attended, 0.0).astype(BF16)
    send(ST_F, "gx", t_f, r_f, False)

    ctile = (iota((256, 128), 0) & 7) >> 1
    received(ST_F, r_f)
    heads16 = r_f[...].astype(F32).reshape(128, 128).astype(BF16)
    cpair = (iota((128, 128), 0) & 7) >> 1

    def project(other):
        rows = mm(sel_g[pl.ds(256 * other, 256)], heads16).astype(BF16)
        sums = mm(jnp.concatenate([rows[0:128], rows[128:256]], axis=1), v_wo[...])
        return pick(cpair, [sums[:, 128 * c : 128 * c + 128] for c in range(3)]).reshape(8, 16, 128)

    s_x[...] = project(1)
    push(ST_X, s_x, r_x, 2 * z + 1 - core)
    mine = project(0)
    pltpu.make_async_copy(r_x, r_x, recv_sem.at[ST_X]).wait()
    s_g[...] = (mine + r_x[...]).astype(BF16)
    over_z(lambda far: push(ST_G, s_g.at[lax.rem(far, 8)], r_g.at[z], 2 * far + core))
    r_g[z] = s_g[low_z]
    received(ST_A, r_a)
    total_a = total(r_a)

    received(ST_G, r_g)
    both = total(r_g)
    tiles = []
    for half in range(2):
        branch = jnp.where(s8 < 6, both[8 * half : 8 * half + 8], 0.0)
        gained = branch * pg
        stream = jnp.where(s8 < 6, r_b[2 * pair + half].astype(F32), 0.0)
        branch_sums = lane_sums(
            [(0, branch * branch), (1, stream * gained), (2, gained * gained)]
            + [(3 + e, gained * rm[e]) for e in range(8)]
        )
        tiles.append(jnp.where(s8 < 6, gained * mg, split_terms(branch_sums)))
        branch_t[half] = gained
    t_j[...] = jnp.concatenate(tiles, axis=0).astype(BF16)
    over_near(lambda p: push(ST_J, t_j, r_j.at[pair], p))
    r_j[pair] = t_j[...]

    received(ST_J, r_j)
    gate_up(r_j[...].astype(F32).reshape(256, 128).astype(BF16), s_k)
    send(ST_K, "gx", s_k, r_k, True)
    received(ST_K, r_k)
    total_k = total(r_k)

    sums_a, sums_k = join_terms(total_a[32:40]), join_terms(total_k[32:40])
    post = lax.rsqrt(sums_k[:, 0:1] / MODEL_WIDTH + EPS)
    stream_square = sums_a[:, 0:1] + 2.0 * post * sums_k[:, 1:2] + post * post * sums_k[:, 2:3]
    pre = lax.rsqrt(stream_square / MODEL_WIDTH + EPS)
    logits = pre * (sums_a + post * sums_k)
    named = (l8 >= 3) & (l8 < 11)
    exponent = jnp.where(named, jnp.exp(jnp.where(named, logits, 0.0)), 0.0)
    chance = exponent / jnp.sum(exponent, axis=1, keepdims=True)
    combine = jnp.sum(jnp.where(l8 == 3 + (s8 >> 1), chance, 0.0), axis=1, keepdims=True)

    def spread(column, first):
        two = [jnp.broadcast_to(column[first + k : first + k + 1], (8, 128)) for k in range(2)]
        return jnp.where((s8 & 1) == 0, two[0], two[1])

    hidden = []
    for e in range(EXP_WIN):
        post_e, pre_e = spread(post, 2 * e), spread(pre, 2 * e)
        gate, up = (
            pre_e * (total_a[16 * e + 8 * u : 16 * e + 8 * u + 8] + post_e * total_k[16 * e + 8 * u : 16 * e + 8 * u + 8])
            for u in range(2)
        )
        bent = 0.5 * gate * (1.0 + jnp.tanh(math.sqrt(2.0 / math.pi) * (gate + 0.044715 * gate * gate * gate)))
        hidden.append(bent * up * spread(combine, 2 * e))
    t_h[...] = jnp.concatenate(hidden, axis=0).astype(BF16)
    send(ST_H, "gx", t_h, r_h, False)

    mixed = as_rows(base_t[...] + spread(post, 4) * branch_t[high])

    received(ST_H, r_h)
    hidden = r_h[...].astype(F32).reshape(256, 128).astype(BF16)
    sums = jnp.zeros((256, 384), F32)
    for e in range(EXP_WIN):
        rows = mm(perm_l[pl.ds(1024 * e, 1024)], hidden).astype(BF16)
        left = jnp.concatenate([rows[256 * ct : 256 * ct + 256] for ct in range(4)], axis=1)
        sums = sums + mm(left, v_wd[e])
    s_l[...] = pick(ctile, [sums[:, 128 * c : 128 * c + 128] for c in range(3)]).reshape(32, 8, 128).astype(BF16)
    send(ST_L, "gy", s_l, r_l, True)
    received(ST_L, r_l)
    res_ref[...] = jnp.concatenate([mixed, as_rows(total(r_l))], axis=0).astype(BF16)

    for stage, dst in (
        (ST_B, r_b), (ST_C, r_c), (ST_D, r_d), (ST_E, r_e), (ST_F, r_f), (ST_G, r_g), (ST_J, r_j), (ST_A, r_a),
        (ST_K, r_k), (ST_H, r_h), (ST_L, r_l),
    ):
        pltpu.make_async_copy(peers_of(dst), peers_of(dst), send_sem.at[stage]).wait()
    pltpu.make_async_copy(s_x, s_x, send_sem.at[ST_X]).wait()


def local(
    residual, attn_gain, wqkv, rotated_key_cache, slot_value_cache, lengths, starts, wo, post_gain, moe_gain, router,
    expert_ids, w_gate_up, w_down,
):
    anywhere = pl.BlockSpec(memory_space=pltpu.HBM)
    scalars = pl.BlockSpec(memory_space=pltpu.SMEM)
    vmem = pltpu.VMEM
    gy_tiles = vmem((NY, 8, 128), BF16)
    gx_tiles = vmem((NX, 8, 128), BF16)
    tile = vmem((8, 128), BF16)
    pairs = vmem((16, 16, 128), BF16)
    result = pl.pallas_call(
        kernel,
        out_shape=pltpu.VMEM((4, 384), BF16),
        in_specs=[anywhere] * 5 + [scalars] * 2 + [anywhere] * 7,
        out_specs=pl.BlockSpec(memory_space=pltpu.VMEM),
        scratch_shapes=[
            vmem((2, 384), BF16), vmem((384,), F32), vmem((384,), F32), vmem((384,), F32), vmem((8, 384), BF16),
            vmem((2, 64), I32), vmem((384, 256), BF16), vmem((4, 64, 1024), BF16), vmem((4, 64, 1024), BF16),
            vmem((256, 384), BF16), vmem((2, 384, 2, 512), BF16), vmem((2, 512, 384), BF16),
            vmem((2, 2, 384, 512), BF16),
            vmem((512, 256), BF16), vmem((256, 256), BF16), vmem((512, 128), BF16), vmem((896, 256), BF16),
            vmem((2048, 256), BF16), vmem((8, 8, 128), F32), vmem((8, 256), F32), vmem((8, 128), F32),
            vmem((2, 8, 128), F32), vmem((32, 8, 128), F32), vmem((256, 128), BF16),
            tile, gy_tiles, vmem((NX, 16, 128), F32), vmem((NX, 16, 128), F32), tile, gy_tiles, gy_tiles, gy_tiles,
            tile, gx_tiles, vmem((8, 16, 128), F32), vmem((8, 16, 128), F32), vmem((8, 16, 128), BF16), pairs,
            vmem((16, 128), BF16), pairs, vmem((NX, 40, 128), BF16), vmem((NX, 40, 128), BF16),
            vmem((NX, 40, 128), BF16), vmem((NX, 40, 128), BF16), vmem((16, 128), BF16), vmem((NX, 16, 128), BF16),
            gy_tiles, gy_tiles,
            pltpu.SemaphoreType.DMA((13,)), pltpu.SemaphoreType.DMA((12,)), pltpu.SemaphoreType.DMA((12,)),
        ],
        compiler_params=pltpu.CompilerParams(
            collective_id=0, has_side_effects=True, vmem_limit_bytes=63 * 1024 * 1024
        ),
        name="decode_step",
    )(
        residual, attn_gain, wqkv, rotated_key_cache, slot_value_cache, lengths, starts, wo,
        post_gain, moe_gain, router.T, expert_ids.T, w_gate_up, w_down,
    )
    return result[:2], result[2:]


def solution(mesh):
    return jax.shard_map(
        local,
        mesh=mesh,
        in_specs=(
            P("gy", "gx"), P("gx"), P("gx", "gy"), P("gx", "gy", None), P("gx", "gy", None), P("gx"), P("gx"),
            P("gy", "gx"), P("gx"), P("gx"), P("gx", None), P(), P(None, "gx", None, "gy"), P(None, "gy", "gx"),
        ),
        out_specs=(P("gy", "gx"), P("gy", "gx")),
        check_vma=False,
    )
```

```python
import functools
import math

import jax
import jax.numpy as jnp
from jax import lax
from jax.experimental import pallas as pl
from jax.experimental.pallas import tpu as pltpu
from jax.sharding import PartitionSpec as P

MODEL_WIDTH = 6144
QUERY_HEADS = 48
KEY_VALUE_HEADS = 8
HEAD_SIZE = 128
WINDOW_SLOTS = 2048
EXP_WIN = 2
NX, NY = 16, 32
EPS = 1e-05
CAP = 30.0
F32, BF16, I32 = jnp.float32, jnp.bfloat16, jnp.int32
MESH = pl.DeviceIdType.MESH

ST_B, ST_C, ST_D, ST_E, ST_F, ST_G, ST_J, ST_A, ST_K, ST_H, ST_L, ST_X = range(12)


def iota(shape, dim):
    return lax.broadcasted_iota(I32, shape, dim)


def onehot(condition):
    return jnp.where(condition, 1.0, 0.0).astype(BF16)


def mm(a, b):
    return jnp.dot(a, b, preferred_element_type=F32)


def pick(number, values):
    result = values[-1]
    for k in range(len(values) - 2, -1, -1):
        result = jnp.where(number == k, values[k], result)
    return result


def gain_tile(gain):
    s = iota((8, 128), 0)
    parts = [jnp.broadcast_to(gain[pl.ds(128 * c, 128)].reshape(1, 128), (8, 128)) for c in range(3)]
    return pick(s >> 1, parts + [jnp.ones((8, 128), F32)])


def fold_requests(v):
    u = v + pltpu.roll(v, 4, 0)
    return u + pltpu.roll(u, 2, 0)


def split_terms(v):
    hi = v.astype(BF16).astype(F32)
    rest = v - hi
    mid = rest.astype(BF16).astype(F32)
    low = rest - mid
    return hi + pltpu.roll(mid, 16, 1) + pltpu.roll(low, 32, 1)


def join_terms(v):
    return v + pltpu.roll(v, 112, 1) + pltpu.roll(v, 96, 1)


def place_of(n):
    return (((n >> 2) & 7) << 2) + (((n >> 1) & 1) << 1) + (n >> 5)


def request_at(index):
    return (((index >> 5) + (((index >> 3) & 1) << 3)) << 2) + (((index >> 4) & 1) << 1) + (index & 1)


def as_rows(tile):
    return jnp.concatenate([tile[0:2], tile[2:4], tile[4:6]], axis=1)


def kernel(
    residual, attn_gain, wqkv, keys, values, lengths, starts, wo, post_gain, moe_gain, router, ids, w_gate_up, w_down,
    res_ref,
    v_res, v_ag, v_pg, v_mg, v_rt, v_ids, v_wqkv, v_keys, v_vals, v_wo, v_gu, v_wd, w_split,
    perm_c, sel_e, sel_g, perm_k, perm_l, rm, mask, base_t, branch_t, q_rows, x_moe,
    t_b, r_b, s_c, r_c, t_d, r_d, s_e, r_e, t_f, r_f, s_x, r_x, s_g, r_g, t_j, r_j, s_a, r_a, s_k, r_k, t_h, r_h, s_l, r_l,
    load_sem, send_sem, recv_sem,
):
    gx = lax.axis_index("gx")
    gy = lax.axis_index("gy")
    z, core = lax.div(gy, 2), lax.rem(gy, 2)
    px, py = lax.div(gx, 4), lax.rem(gx, 4)
    low_z, high = lax.rem(z, 8), lax.div(z, 8)
    pair = 2 * low_z + core
    place = 2 * pair + high

    def over_gy(act):
        def body(q, carry):
            h = lax.div(q + 1, 2)
            far = lax.rem(z + 8 + h * (1 - 2 * lax.rem(q, 2)), 16)
            act(2 * far + core)
            act(2 * far + 1 - core)
            return carry

        lax.fori_loop(0, 15, body, 0, unroll=True)
        act(2 * z + 1 - core)

    def over_gx(act):
        def shift(t):
            return lax.rem(10 - lax.div(t * (t + 1), 2), 4)

        def body(k, carry):
            qx = lax.rem(px + shift(lax.div(k, 4)), 4)
            qy = lax.rem(py + shift(lax.rem(k, 4)), 4)
            act(4 * qx + qy)
            return carry

        lax.fori_loop(0, 15, body, 0, unroll=True)

    barrier = pltpu.get_barrier_semaphore()
    over_gy(lambda p: pl.semaphore_signal(barrier, inc=1, device_id=(gx, p), device_id_type=MESH))
    over_gx(lambda p: pl.semaphore_signal(barrier, inc=1, device_id=(p, gy), device_id_type=MESH))

    loads = []

    def load(src, dst, k):
        c = pltpu.make_async_copy(src, dst, load_sem.at[k])
        c.start()
        loads.append(c)

    load(residual, v_res, 0)
    load(attn_gain, v_ag, 1)
    load(post_gain, v_pg, 2)
    load(moe_gain, v_mg, 3)
    load(router, v_rt, 4)
    load(ids, v_ids, 5)
    load(wqkv, v_wqkv, 6)
    load(keys, v_keys, 7)
    load(values, v_vals, 8)
    load(wo.at[pl.ds(pl.multiple_of(64 * core, 64), 128)], v_wo.at[pl.ds(0, 128)], 9)
    load(
        wo.at[pl.ds(pl.multiple_of(128 * (1 - core), 64), 64)],
        v_wo.at[pl.ds(pl.multiple_of(128 + 64 * core, 64), 64)],
        10,
    )
    load(w_gate_up, v_gu, 11)
    load(w_down, v_wd, 12)

    def send(stage, along, src, dst, each):
        me = gy if along == "gy" else gx

        def act(p):
            pltpu.make_async_remote_copy(
                src_ref=src.at[p] if each else src,
                dst_ref=dst.at[me],
                send_sem=send_sem.at[stage],
                recv_sem=recv_sem.at[stage],
                device_id=(gx, p) if along == "gy" else (p, gy),
                device_id_type=MESH,
            ).start()

        (over_gy if along == "gy" else over_gx)(act)
        dst[me] = src[me] if each else src[...]

    def over_z(act):
        def body(q, carry):
            h = lax.div(q + 1, 2)
            act(lax.rem(z + 8 + h * (1 - 2 * lax.rem(q, 2)), 16))
            return carry

        lax.fori_loop(0, 15, body, 0, unroll=True)

    def over_near(act):
        def body(q, carry):
            h = lax.div(q + 1, 2)
            near = lax.rem(z + 16 + (4 - h) * (2 * lax.rem(q, 2) - 1), 16)
            act(2 * near + core)
            act(2 * near + 1 - core)
            return carry

        lax.fori_loop(0, 7, body, 0, unroll=True)
        act(2 * z + 1 - core)

    def push(stage, src, dst, p):
        pltpu.make_async_remote_copy(
            src_ref=src,
            dst_ref=dst,
            send_sem=send_sem.at[stage],
            recv_sem=recv_sem.at[stage],
            device_id=(gx, p),
            device_id_type=MESH,
        ).start()

    def peers_of(dst):
        return dst.at[pl.ds(0, dst.shape[0] - 1)]

    def received(stage, dst):
        pltpu.make_async_copy(peers_of(dst), peers_of(dst), recv_sem.at[stage]).wait()

    def total(ref):
        return jnp.sum(ref[...].astype(F32), axis=0)

    s8, l8 = iota((8, 128), 0), iota((8, 128), 1)
    for c in loads[:6]:
        c.wait()
    res = v_res[...].astype(F32)
    base = jnp.concatenate([res[:, 0:128], res[:, 128:256], res[:, 256:384], jnp.zeros((2, 128), F32)], axis=0)
    base_t[...] = base
    ag, pg, mg = gain_tile(v_ag), gain_tile(v_pg), gain_tile(v_mg)
    rt = v_rt[...].astype(F32)
    for e in range(8):
        row = rt[e : e + 1]
        parts = [jnp.broadcast_to(row[:, 128 * c : 128 * c + 128], (8, 128)) for c in range(3)]
        rm[e] = pick(s8 >> 1, parts + [jnp.zeros((8, 128), F32)]) * mg

    def lane_sums(terms):
        acc = jnp.zeros((8, 128), F32)
        for k, term in terms:
            acc = jnp.where(l8 == k, jnp.sum(term, axis=1, keepdims=True), acc)
        return fold_requests(acc)

    base_sums = lane_sums([(0, base * base)] + [(3 + e, base * rm[e]) for e in range(8)])
    t_b[...] = jnp.where(s8 < 6, base, split_terms(base_sums)).astype(BF16)

    row, lane = iota((512, 256), 0), iota((512, 256), 1)
    n = 4 * ((row >> 3) & 15) + (row & 3)
    perm_c[...] = onehot(lane == (place_of(n) << 3) + 2 * (row >> 7) + (n & 1))

    pl.semaphore_wait(barrier, NX + NY - 2)
    over_gy(lambda p: push(ST_B, t_b, r_b.at[place], p))
    r_b[place] = t_b[...]

    row, lane = iota((256, 256), 0), iota((256, 256), 1)
    j, t = row >> 3, (row >> 2) & 1
    head = 3 * (j >> 1) + jnp.where(t == 1, 1, 2 * (j & 1))
    sel_e[...] = onehot(lane == ((head >> 1) << 3) + ((head & 1) << 2) + (row & 3))

    row, lane = iota((512, 128), 0), iota((512, 128), 1)
    s = row & 7
    n = ((((row >> 4) & 7) + (((row >> 3) & 1) << 3)) << 2) + 2 * (core + (row >> 8) * (1 - 2 * core)) + (s & 1)
    sel_g[...] = onehot((lane == ((n >> 2) << 3) + (((row >> 7) & 1) << 2) + (n & 3)) & (s < 6))

    lane_code, row_code = [], []
    id_rows = v_ids[...]
    for e in range(EXP_WIN):
        picked = jnp.where((id_rows[0:1] == e) | (id_rows[1:2] == e), 1.0, 0.0)
        a, b = iota((64, 64), 0), iota((64, 64), 1)
        column = jnp.sum(jnp.where(a == b, picked, 0.0), axis=1, keepdims=True)
        a, b = iota((64, 256), 0), iota((64, 256), 1)
        of = request_at(b)
        before = jnp.sum(jnp.where(a < of, column, 0.0), axis=0, keepdims=True)
        named = jnp.sum(jnp.where(a == of, column, 0.0), axis=0, keepdims=True)
        lane_code.append(jnp.where(named > 0.5, before, -1.0))
        a, b = iota((256, 64), 0), iota((256, 64), 1)
        of = 4 * ((z + 5 + (a >> 4)) & 15) + 2 * ((a >> 3) & 1) + (a & 1)
        before = jnp.sum(jnp.where(b < of, picked, 0.0), axis=1, keepdims=True)
        named = jnp.sum(jnp.where(b == of, picked, 0.0), axis=1, keepdims=True)
        row_code.append(jnp.where(named > 0.5, before, -1.0))

    row, lane = iota((128, 256), 0), iota((128, 256), 1)
    q, s = row & 7, lane & 7
    slot = (2 * (row >> 3) + (row & 1)).astype(F32)
    for e in range(EXP_WIN):
        here = slot == lane_code[e]
        for c in range(3):
            perm_k[pl.ds((3 * e + c) * 128, 128)] = onehot(here & ((s >> 1) == c))
    sums_here = (
        ((q >> 1) == 0) & (slot == lane_code[0]) | ((q >> 1) == 1) & (slot == lane_code[1])
    ) & ((s >> 1) == 3)
    own = ((q >> 1) == 2) & (lane == 8 * place + 6 + (q & 1))
    perm_k[pl.ds(768, 128)] = onehot(sums_here | own)

    row, lane = iota((256, 256), 0), iota((256, 256), 1)
    slot = (2 * (lane >> 4) + (lane & 1)).astype(F32)
    for e in range(EXP_WIN):
        here = (slot == row_code[e]) & (((lane >> 3) & 1) == e) & ((row & 7) < 6)
        for ct in range(4):
            block = onehot(here & (((lane >> 1) & 3) == ct))
            for part in range(2):
                perm_l[pl.ds(1024 * part + 512 * e + 128 * ct, 128)] = block[128 * part : 128 * part + 128]

    row, lane = iota((8, 256), 0), iota((8, 256), 1)
    last = pick(lane >> 6, [lengths[r] for r in range(4)]) - 1
    first = pick(lane >> 6, [starts[r] for r in range(4)])
    position = last - ((last - (64 * gy + (lane & 63))) & (WINDOW_SLOTS - 1))
    usable = (position >= jnp.maximum(first, last - (WINDOW_SLOTS - 2))) & ((lane >> 6) == (row & 3))
    mask[...] = jnp.where(usable, 1.0, 0.0)

    turn = (l8 & 63).astype(F32)
    angle = pick(s8 & 3, [lengths[r] for r in range(4)]).astype(F32) * jnp.exp(turn * (-2.0 * math.log(10000.0) / 128))
    rotated = 2 * gy < QUERY_HEADS + KEY_VALUE_HEADS
    cosine = jnp.where(rotated, jnp.cos(angle), 1.0)
    sine = jnp.where(rotated, jnp.where(l8 < 64, -1.0, 1.0) * jnp.sin(angle), 0.0)

    v_wo[pl.ds(pl.multiple_of(192 - 64 * core, 64), 64)] = jnp.zeros((64, 384), BF16)
    loads[6].wait()

    received(ST_B, r_b)
    x = r_b[...].astype(F32)
    rows = mm(perm_c[...], (x * ag).reshape(256, 128).astype(BF16))
    left = jnp.concatenate([rows[128 * c : 128 * c + 128] for c in range(3)], axis=1).astype(BF16)
    sums = mm(left, v_wqkv[...])
    hh = (iota((128, 128), 0) >> 2) & 1
    sums = jnp.where(hh == 0, sums[:, 0:128], sums[:, 128:256])
    s_c[...] = jnp.concatenate([sums.reshape(16, 8, 128), rows[384:512].reshape(16, 8, 128)], axis=1)
    send(ST_C, "gx", s_c, r_c, True)
    x_moe[...] = (x * mg).reshape(256, 128).astype(BF16)
    for c in loads[11:12]:
        c.wait()
    for e in range(EXP_WIN):
        for u in range(2):
            w_split[e, u] = v_gu[e, :, u, :]

    received(ST_C, r_c)
    both = total(r_c)
    square = join_terms(both[8:16])
    scale = lax.rsqrt(square[:, 0:1] / MODEL_WIDTH + EPS)
    heads = both[0:8] * scale
    heads = heads * cosine + pltpu.roll(heads, 64, 1) * sine
    t_d[...] = heads.astype(BF16)
    send(ST_D, "gy", t_d, r_d, False)

    def gate_up(x_rows, out):
        rows = mm(perm_k[...], x_rows)
        rows16 = rows.astype(BF16)
        ct = (iota((128, 128), 0) & 7) >> 1
        for e in range(EXP_WIN):
            left = jnp.concatenate([rows16[(3 * e + c) * 128 : (3 * e + c) * 128 + 128] for c in range(3)], axis=1)
            halves = []
            for u in range(2):
                full = mm(left, w_split[e, u])
                halves.append(pick(ct, [full[:, 128 * k : 128 * k + 128] for k in range(4)]).reshape(16, 8, 128))
            out[:, pl.ds(16 * e, 16), :] = jnp.concatenate(halves, axis=1).astype(BF16)
        sums = rows[768:896].reshape(16, 8, 128)
        out[:, pl.ds(32, 8), :] = sums.astype(BF16)

    gate_up(x_moe[...], s_a)
    send(ST_A, "gx", s_a, r_a, True)
    for c in loads[7:11] + loads[12:13]:
        c.wait()

    received(ST_D, r_d)
    everything = r_d[...].astype(F32).reshape(256, 128).astype(BF16)
    queries = mm(sel_e[...], everything)
    q_rows[...] = queries.reshape(32, 8, 128)
    queries = queries.astype(BF16)
    scores = []
    for g in range(KEY_VALUE_HEADS):
        kg = v_keys[:, :, pl.ds(128 * g, 128)].reshape(256, 128)
        scores.append(
            lax.dot_general(
                queries[32 * g : 32 * g + 32], kg, (((1,), (1,)), ((), ())), preferred_element_type=F32
            )
        )
    score = jnp.concatenate(scores, axis=0)
    weight = jnp.exp(CAP * jnp.tanh(score * (HEAD_SIZE**-0.5 / CAP))).reshape(32, 8, 256) * mask[...]
    weight = weight.reshape(256, 256)
    weight16 = weight.astype(BF16)
    sums = []
    for g in range(KEY_VALUE_HEADS):
        vg = v_vals[:, :, pl.ds(128 * g, 128)].reshape(256, 128)
        sums.append(mm(weight16[32 * g : 32 * g + 32], vg))
    summed = jnp.concatenate(sums, axis=0)
    total1 = jnp.broadcast_to(jnp.sum(weight, axis=1, keepdims=True), (256, 128))
    total0 = pltpu.roll(total1, 4, 0)
    row, lane = iota((256, 128), 0), iota((256, 128), 1)
    low1 = total1 - total1.astype(BF16).astype(F32)
    low0 = total0 - total0.astype(BF16).astype(F32)
    free = pick((lane & 63) >> 4, [total1, low1, total0, low0])
    keep = (((row >> 2) & 1) == 0) | ((lane >> 6) == ((row >> 3) & 1))
    s_e[...] = jnp.where(keep, summed, free).reshape(32, 8, 128).astype(BF16)
    send(ST_E, "gy", s_e, r_e, True)

    group = lax.div(gy, 4)
    second = lax.rem(group, 2)

    def fresh(first_block):
        tile = r_d[first_block + lax.div(group, 2)].astype(F32)
        return jnp.where((s8 >> 2) == second, tile, pltpu.roll(tile, 4, 0))

    own_query = q_rows[gy].astype(BF16).astype(F32)
    own_score = jnp.sum(own_query * fresh(24), axis=1, keepdims=True) * (HEAD_SIZE**-0.5 / CAP)
    own_weight = jnp.exp(CAP * jnp.tanh(own_score))
    own_value = own_weight.astype(BF16).astype(F32) * fresh(28)

    received(ST_E, r_e)
    tile = total(r_e)
    half = (l8 >> 6) == core
    quarter = (l8 & 63) >> 5
    den1 = jnp.sum(jnp.where(~half & (quarter == 0), tile, 0.0), axis=1, keepdims=True) * 0.0625
    den0 = jnp.sum(jnp.where(~half & (quarter == 1), tile, 0.0), axis=1, keepdims=True) * 0.0625
    den1, den0 = jnp.broadcast_to(den1, (8, 128)), jnp.broadcast_to(den0, (8, 128))
    den = jnp.where(s8 < 4, pltpu.roll(den0, 4, 0), den1) + own_weight
    attended = (tile + own_value) / den
    t_f[...] = jnp.where((s8 < 4) | half, attended, 0.0).astype(BF16)
    send(ST_F, "gx", t_f, r_f, False)

    ctile = (iota((256, 128), 0) & 7) >> 1
    received(ST_F, r_f)
    heads16 = r_f[...].astype(F32).reshape(128, 128).astype(BF16)
    cpair = (iota((128, 128), 0) & 7) >> 1

    def project(other):
        rows = mm(sel_g[pl.ds(256 * other, 256)], heads16).astype(BF16)
        sums = mm(jnp.concatenate([rows[0:128], rows[128:256]], axis=1), v_wo[...])
        return pick(cpair, [sums[:, 128 * c : 128 * c + 128] for c in range(3)]).reshape(8, 16, 128)

    s_x[...] = project(1)
    push(ST_X, s_x, r_x, 2 * z + 1 - core)
    mine = project(0)
    pltpu.make_async_copy(r_x, r_x, recv_sem.at[ST_X]).wait()
    s_g[...] = (mine + r_x[...]).astype(BF16)
    over_z(lambda far: push(ST_G, s_g.at[lax.rem(far, 8)], r_g.at[z], 2 * far + core))
    r_g[z] = s_g[low_z]
    received(ST_A, r_a)
    total_a = total(r_a)

    received(ST_G, r_g)
    both = total(r_g)
    tiles = []
    for half in range(2):
        branch = jnp.where(s8 < 6, both[8 * half : 8 * half + 8], 0.0)
        gained = branch * pg
        stream = jnp.where(s8 < 6, r_b[2 * pair + half].astype(F32), 0.0)
        branch_sums = lane_sums(
            [(0, branch * branch), (1, stream * gained), (2, gained * gained)]
            + [(3 + e, gained * rm[e]) for e in range(8)]
        )
        tiles.append(jnp.where(s8 < 6, gained * mg, split_terms(branch_sums)))
        branch_t[half] = gained
    t_j[...] = jnp.concatenate(tiles, axis=0).astype(BF16)
    over_near(lambda p: push(ST_J, t_j, r_j.at[pair], p))
    r_j[pair] = t_j[...]

    received(ST_J, r_j)
    gate_up(r_j[...].astype(F32).reshape(256, 128).astype(BF16), s_k)
    send(ST_K, "gx", s_k, r_k, True)
    received(ST_K, r_k)
    total_k = total(r_k)

    sums_a, sums_k = join_terms(total_a[32:40]), join_terms(total_k[32:40])
    post = lax.rsqrt(sums_k[:, 0:1] / MODEL_WIDTH + EPS)
    stream_square = sums_a[:, 0:1] + 2.0 * post * sums_k[:, 1:2] + post * post * sums_k[:, 2:3]
    pre = lax.rsqrt(stream_square / MODEL_WIDTH + EPS)
    logits = pre * (sums_a + post * sums_k)
    named = (l8 >= 3) & (l8 < 11)
    exponent = jnp.where(named, jnp.exp(jnp.where(named, logits, 0.0)), 0.0)
    chance = exponent / jnp.sum(exponent, axis=1, keepdims=True)
    combine = jnp.sum(jnp.where(l8 == 3 + (s8 >> 1), chance, 0.0), axis=1, keepdims=True)

    def spread(column, first):
        two = [jnp.broadcast_to(column[first + k : first + k + 1], (8, 128)) for k in range(2)]
        return jnp.where((s8 & 1) == 0, two[0], two[1])

    hidden = []
    for e in range(EXP_WIN):
        post_e, pre_e = spread(post, 2 * e), spread(pre, 2 * e)
        gate, up = (
            pre_e * (total_a[16 * e + 8 * u : 16 * e + 8 * u + 8] + post_e * total_k[16 * e + 8 * u : 16 * e + 8 * u + 8])
            for u in range(2)
        )
        bent = 0.5 * gate * (1.0 + jnp.tanh(math.sqrt(2.0 / math.pi) * (gate + 0.044715 * gate * gate * gate)))
        hidden.append(bent * up * spread(combine, 2 * e))
    t_h[...] = jnp.concatenate(hidden, axis=0).astype(BF16)
    send(ST_H, "gx", t_h, r_h, False)

    mixed = as_rows(base_t[...] + spread(post, 4) * branch_t[high])

    received(ST_H, r_h)
    hidden = r_h[...].astype(F32).reshape(256, 128).astype(BF16)
    chalf = (iota((128, 128), 0) & 7) >> 1

    def expert_sums(part):
        sums = jnp.zeros((128, 384), F32)
        for e in range(EXP_WIN):
            rows = mm(perm_l[pl.ds(1024 * part + 512 * e, 512)], hidden).astype(BF16)
            left = jnp.concatenate([rows[128 * ct : 128 * ct + 128] for ct in range(4)], axis=1)
            sums = sums + mm(left, v_wd[e])
        blocks = pick(chalf, [sums[:, 128 * c : 128 * c + 128] for c in range(3)])
        s_l[pl.ds(16 * part, 16)] = blocks.reshape(16, 8, 128).astype(BF16)

    def send_sums(k):
        chip = lax.rem(z + 5 + k, 16)
        for other in range(2):
            push(ST_L, s_l.at[2 * k + other], r_l.at[gy], 2 * chip + other)

    expert_sums(0)

    def far_chips(q, carry):
        h = lax.div(q + 1, 2)
        send_sums(3 + h * (1 - 2 * lax.rem(q, 2)))
        return carry

    lax.fori_loop(0, 7, far_chips, 0, unroll=True)
    send_sums(7)
    expert_sums(1)

    def near_chips(k, carry):
        send_sums(k)
        return carry

    lax.fori_loop(8, 11, near_chips, 0, unroll=True)
    lax.fori_loop(12, 16, near_chips, 0, unroll=True)
    push(ST_L, s_l.at[23 - core], r_l.at[gy], 2 * z + 1 - core)
    r_l[gy] = s_l[22 + core]
    received(ST_L, r_l)
    res_ref[...] = jnp.concatenate([mixed, as_rows(total(r_l))], axis=0).astype(BF16)

    for stage, dst in (
        (ST_B, r_b), (ST_C, r_c), (ST_D, r_d), (ST_E, r_e), (ST_F, r_f), (ST_G, r_g), (ST_J, r_j), (ST_A, r_a),
        (ST_K, r_k), (ST_H, r_h), (ST_L, r_l),
    ):
        pltpu.make_async_copy(peers_of(dst), peers_of(dst), send_sem.at[stage]).wait()
    pltpu.make_async_copy(s_x, s_x, send_sem.at[ST_X]).wait()


def local(
    residual, attn_gain, wqkv, rotated_key_cache, slot_value_cache, lengths, starts, wo, post_gain, moe_gain, router,
    expert_ids, w_gate_up, w_down,
):
    anywhere = pl.BlockSpec(memory_space=pltpu.HBM)
    scalars = pl.BlockSpec(memory_space=pltpu.SMEM)
    vmem = pltpu.VMEM
    gy_tiles = vmem((NY, 8, 128), BF16)
    gx_tiles = vmem((NX, 8, 128), BF16)
    tile = vmem((8, 128), BF16)
    pairs = vmem((16, 16, 128), BF16)
    result = pl.pallas_call(
        kernel,
        out_shape=pltpu.VMEM((4, 384), BF16),
        in_specs=[anywhere] * 5 + [scalars] * 2 + [anywhere] * 7,
        out_specs=pl.BlockSpec(memory_space=pltpu.VMEM),
        scratch_shapes=[
            vmem((2, 384), BF16), vmem((384,), F32), vmem((384,), F32), vmem((384,), F32), vmem((8, 384), BF16),
            vmem((2, 64), I32), vmem((384, 256), BF16), vmem((4, 64, 1024), BF16), vmem((4, 64, 1024), BF16),
            vmem((256, 384), BF16), vmem((2, 384, 2, 512), BF16), vmem((2, 512, 384), BF16),
            vmem((2, 2, 384, 512), BF16),
            vmem((512, 256), BF16), vmem((256, 256), BF16), vmem((512, 128), BF16), vmem((896, 256), BF16),
            vmem((2048, 256), BF16), vmem((8, 8, 128), F32), vmem((8, 256), F32), vmem((8, 128), F32),
            vmem((2, 8, 128), F32), vmem((32, 8, 128), F32), vmem((256, 128), BF16),
            tile, gy_tiles, vmem((NX, 16, 128), F32), vmem((NX, 16, 128), F32), tile, gy_tiles, gy_tiles, gy_tiles,
            tile, gx_tiles, vmem((8, 16, 128), F32), vmem((8, 16, 128), F32), vmem((8, 16, 128), BF16), pairs,
            vmem((16, 128), BF16), pairs, vmem((NX, 40, 128), BF16), vmem((NX, 40, 128), BF16),
            vmem((NX, 40, 128), BF16), vmem((NX, 40, 128), BF16), vmem((16, 128), BF16), vmem((NX, 16, 128), BF16),
            gy_tiles, gy_tiles,
            pltpu.SemaphoreType.DMA((13,)), pltpu.SemaphoreType.DMA((12,)), pltpu.SemaphoreType.DMA((12,)),
        ],
        compiler_params=pltpu.CompilerParams(
            collective_id=0, has_side_effects=True, vmem_limit_bytes=63 * 1024 * 1024
        ),
        name="decode_step",
    )(
        residual, attn_gain, wqkv, rotated_key_cache, slot_value_cache, lengths, starts, wo,
        post_gain, moe_gain, router.T, expert_ids.T, w_gate_up, w_down,
    )
    return result[:2], result[2:]


def solution(mesh):
    return jax.shard_map(
        local,
        mesh=mesh,
        in_specs=(
            P("gy", "gx"), P("gx"), P("gx", "gy"), P("gx", "gy", None), P("gx", "gy", None), P("gx"), P("gx"),
            P("gy", "gx"), P("gx"), P("gx"), P("gx", None), P(), P(None, "gx", None, "gy"), P(None, "gy", "gx"),
        ),
        out_specs=(P("gy", "gx"), P("gy", "gx")),
        check_vma=False,
    )
```

```python
import functools
import math

import jax
import jax.numpy as jnp
from jax import lax
from jax.experimental import pallas as pl
from jax.experimental.pallas import tpu as pltpu
from jax.sharding import PartitionSpec as P

MODEL_WIDTH = 6144
QUERY_HEADS = 48
KEY_VALUE_HEADS = 8
HEAD_SIZE = 128
WINDOW_SLOTS = 2048
EXP_WIN = 2
NX, NY = 16, 32
EPS = 1e-05
CAP = 30.0
F32, BF16, I32 = jnp.float32, jnp.bfloat16, jnp.int32
MESH = pl.DeviceIdType.MESH

ST_B, ST_C, ST_D, ST_E, ST_F, ST_G, ST_J, ST_A, ST_K, ST_H, ST_L, ST_X = range(12)


def iota(shape, dim):
    return lax.broadcasted_iota(I32, shape, dim)


def onehot(condition):
    return jnp.where(condition, 1.0, 0.0).astype(BF16)


def mm(a, b):
    return jnp.dot(a, b, preferred_element_type=F32)


def pick(number, values):
    result = values[-1]
    for k in range(len(values) - 2, -1, -1):
        result = jnp.where(number == k, values[k], result)
    return result


def gain_tile(gain):
    s = iota((8, 128), 0)
    parts = [jnp.broadcast_to(gain[pl.ds(128 * c, 128)].reshape(1, 128), (8, 128)) for c in range(3)]
    return pick(s >> 1, parts + [jnp.ones((8, 128), F32)])


def fold_requests(v):
    u = v + pltpu.roll(v, 4, 0)
    return u + pltpu.roll(u, 2, 0)


def split_terms(v):
    hi = v.astype(BF16).astype(F32)
    rest = v - hi
    mid = rest.astype(BF16).astype(F32)
    low = rest - mid
    return hi + pltpu.roll(mid, 16, 1) + pltpu.roll(low, 32, 1)


def join_terms(v):
    return v + pltpu.roll(v, 112, 1) + pltpu.roll(v, 96, 1)


def place_of(n):
    return (((n >> 2) & 7) << 2) + (((n >> 1) & 1) << 1) + (n >> 5)


def request_at(index):
    return (((index >> 5) + (((index >> 3) & 1) << 3)) << 2) + (((index >> 4) & 1) << 1) + (index & 1)


def as_rows(tile):
    return jnp.concatenate([tile[0:2], tile[2:4], tile[4:6]], axis=1)


def kernel(
    residual, attn_gain, wqkv, keys, values, lengths, starts, wo, post_gain, moe_gain, router, ids, w_gate_up, w_down,
    res_ref,
    v_res, v_ag, v_pg, v_mg, v_rt, v_ids, v_wqkv, v_keys, v_vals, v_wo, v_gu, v_wd, w_split,
    perm_c, sel_e, sel_g, perm_k, perm_l, rm, mask, base_t, branch_t, q_rows, q_bits, x_moe,
    t_b, r_b, s_c, r_c, t_d, r_d, s_e, r_e, t_f, r_f, s_x, r_x, s_g, r_g, t_j, r_j, s_a, r_a, s_k, r_k, t_h, r_h, s_l, r_l,
    load_sem, send_sem, recv_sem,
):
    gx = lax.axis_index("gx")
    gy = lax.axis_index("gy")
    z, core = lax.div(gy, 2), lax.rem(gy, 2)
    px, py = lax.div(gx, 4), lax.rem(gx, 4)
    low_z, high = lax.rem(z, 8), lax.div(z, 8)
    pair = 2 * low_z + core
    place = 2 * pair + high

    def over_gy(act):
        def body(q, carry):
            h = lax.div(q + 1, 2)
            far = lax.rem(z + 8 + h * (1 - 2 * lax.rem(q, 2)), 16)
            act(2 * far + core)
            act(2 * far + 1 - core)
            return carry

        lax.fori_loop(0, 15, body, 0, unroll=True)
        act(2 * z + 1 - core)

    def over_gx(act):
        def shift(t):
            return lax.rem(10 - lax.div(t * (t + 1), 2), 4)

        def body(k, carry):
            qx = lax.rem(px + shift(lax.div(k, 4)), 4)
            qy = lax.rem(py + shift(lax.rem(k, 4)), 4)
            act(4 * qx + qy)
            return carry

        lax.fori_loop(0, 15, body, 0, unroll=True)

    barrier = pltpu.get_barrier_semaphore()
    over_gy(lambda p: pl.semaphore_signal(barrier, inc=1, device_id=(gx, p), device_id_type=MESH))
    over_gx(lambda p: pl.semaphore_signal(barrier, inc=1, device_id=(p, gy), device_id_type=MESH))

    loads = []

    def load(src, dst, k):
        c = pltpu.make_async_copy(src, dst, load_sem.at[k])
        c.start()
        loads.append(c)

    load(residual, v_res, 0)
    load(attn_gain, v_ag, 1)
    load(post_gain, v_pg, 2)
    load(moe_gain, v_mg, 3)
    load(router, v_rt, 4)
    load(ids, v_ids, 5)
    load(wqkv, v_wqkv, 6)
    load(keys, v_keys, 7)
    load(values, v_vals, 8)
    load(wo.at[pl.ds(pl.multiple_of(64 * core, 64), 128)], v_wo.at[pl.ds(0, 128)], 9)
    load(
        wo.at[pl.ds(pl.multiple_of(128 * (1 - core), 64), 64)],
        v_wo.at[pl.ds(pl.multiple_of(128 + 64 * core, 64), 64)],
        10,
    )
    load(w_gate_up, v_gu, 11)
    load(w_down, v_wd, 12)

    def send(stage, along, src, dst, each):
        me = gy if along == "gy" else gx

        def act(p):
            pltpu.make_async_remote_copy(
                src_ref=src.at[p] if each else src,
                dst_ref=dst.at[me],
                send_sem=send_sem.at[stage],
                recv_sem=recv_sem.at[stage],
                device_id=(gx, p) if along == "gy" else (p, gy),
                device_id_type=MESH,
            ).start()

        (over_gy if along == "gy" else over_gx)(act)
        dst[me] = src[me] if each else src[...]

    def over_z(act):
        def body(q, carry):
            h = lax.div(q + 1, 2)
            act(lax.rem(z + 8 + h * (1 - 2 * lax.rem(q, 2)), 16))
            return carry

        lax.fori_loop(0, 15, body, 0, unroll=True)

    def over_near(act):
        def body(q, carry):
            h = lax.div(q + 1, 2)
            near = lax.rem(z + 16 + (4 - h) * (2 * lax.rem(q, 2) - 1), 16)
            act(2 * near + core)
            act(2 * near + 1 - core)
            return carry

        lax.fori_loop(0, 7, body, 0, unroll=True)
        act(2 * z + 1 - core)

    def push(stage, src, dst, p):
        pltpu.make_async_remote_copy(
            src_ref=src,
            dst_ref=dst,
            send_sem=send_sem.at[stage],
            recv_sem=recv_sem.at[stage],
            device_id=(gx, p),
            device_id_type=MESH,
        ).start()

    def peers_of(dst):
        return dst.at[pl.ds(0, dst.shape[0] - 1)]

    def received(stage, dst):
        pltpu.make_async_copy(peers_of(dst), peers_of(dst), recv_sem.at[stage]).wait()

    def total(ref):
        return jnp.sum(ref[...].astype(F32), axis=0)

    s8, l8 = iota((8, 128), 0), iota((8, 128), 1)
    for c in loads[:6]:
        c.wait()
    res = v_res[...].astype(F32)
    base = jnp.concatenate([res[:, 0:128], res[:, 128:256], res[:, 256:384], jnp.zeros((2, 128), F32)], axis=0)
    base_t[...] = base
    ag, pg, mg = gain_tile(v_ag), gain_tile(v_pg), gain_tile(v_mg)
    rt = v_rt[...].astype(F32)
    for e in range(8):
        row = rt[e : e + 1]
        parts = [jnp.broadcast_to(row[:, 128 * c : 128 * c + 128], (8, 128)) for c in range(3)]
        rm[e] = pick(s8 >> 1, parts + [jnp.zeros((8, 128), F32)]) * mg

    def lane_sums(terms):
        acc = jnp.zeros((8, 128), F32)
        for k, term in terms:
            acc = jnp.where(l8 == k, jnp.sum(term, axis=1, keepdims=True), acc)
        return fold_requests(acc)

    base_sums = lane_sums([(0, base * base)] + [(3 + e, base * rm[e]) for e in range(8)])
    t_b[...] = jnp.where(s8 < 6, base, split_terms(base_sums)).astype(BF16)

    row, lane = iota((512, 256), 0), iota((512, 256), 1)
    n = 4 * ((row >> 3) & 15) + (row & 3)
    perm_c[...] = onehot(lane == (place_of(n) << 3) + 2 * (row >> 7) + (n & 1))

    pl.semaphore_wait(barrier, NX + NY - 2)
    over_gy(lambda p: push(ST_B, t_b, r_b.at[place], p))
    r_b[place] = t_b[...]

    row, lane = iota((256, 256), 0), iota((256, 256), 1)
    j, t = row >> 3, (row >> 2) & 1
    head = 3 * (j >> 1) + jnp.where(t == 1, 1, 2 * (j & 1))
    sel_e[...] = onehot(lane == ((head >> 1) << 3) + ((head & 1) << 2) + (row & 3))

    row, lane = iota((512, 128), 0), iota((512, 128), 1)
    s = row & 7
    n = ((((row >> 4) & 7) + (((row >> 3) & 1) << 3)) << 2) + 2 * (core + (row >> 8) * (1 - 2 * core)) + (s & 1)
    sel_g[...] = onehot((lane == ((n >> 2) << 3) + (((row >> 7) & 1) << 2) + (n & 3)) & (s < 6))

    lane_code, row_code = [], []
    id_rows = v_ids[...]
    for e in range(EXP_WIN):
        picked = jnp.where((id_rows[0:1] == e) | (id_rows[1:2] == e), 1.0, 0.0)
        a, b = iota((64, 64), 0), iota((64, 64), 1)
        column = jnp.sum(jnp.where(a == b, picked, 0.0), axis=1, keepdims=True)
        a, b = iota((64, 256), 0), iota((64, 256), 1)
        of = request_at(b)
        before = jnp.sum(jnp.where(a < of, column, 0.0), axis=0, keepdims=True)
        named = jnp.sum(jnp.where(a == of, column, 0.0), axis=0, keepdims=True)
        lane_code.append(jnp.where(named > 0.5, before, -1.0))
        a, b = iota((256, 64), 0), iota((256, 64), 1)
        of = 4 * ((z + 5 + (a >> 4)) & 15) + 2 * ((a >> 3) & 1) + (a & 1)
        before = jnp.sum(jnp.where(b < of, picked, 0.0), axis=1, keepdims=True)
        named = jnp.sum(jnp.where(b == of, picked, 0.0), axis=1, keepdims=True)
        row_code.append(jnp.where(named > 0.5, before, -1.0))

    row, lane = iota((128, 256), 0), iota((128, 256), 1)
    q, s = row & 7, lane & 7
    slot = (2 * (row >> 3) + (row & 1)).astype(F32)
    for e in range(EXP_WIN):
        here = slot == lane_code[e]
        for c in range(3):
            perm_k[pl.ds((3 * e + c) * 128, 128)] = onehot(here & ((s >> 1) == c))
    sums_here = (
        ((q >> 1) == 0) & (slot == lane_code[0]) | ((q >> 1) == 1) & (slot == lane_code[1])
    ) & ((s >> 1) == 3)
    own = ((q >> 1) == 2) & (lane == 8 * place + 6 + (q & 1))
    perm_k[pl.ds(768, 128)] = onehot(sums_here | own)

    row, lane = iota((256, 256), 0), iota((256, 256), 1)
    slot = (2 * (lane >> 4) + (lane & 1)).astype(F32)
    for e in range(EXP_WIN):
        here = (slot == row_code[e]) & (((lane >> 3) & 1) == e) & ((row & 7) < 6)
        for ct in range(4):
            block = onehot(here & (((lane >> 1) & 3) == ct))
            for part in range(2):
                perm_l[pl.ds(1024 * part + 512 * e + 128 * ct, 128)] = block[128 * part : 128 * part + 128]

    row, lane = iota((8, 256), 0), iota((8, 256), 1)
    last = pick(lane >> 6, [lengths[r] for r in range(4)]) - 1
    first = pick(lane >> 6, [starts[r] for r in range(4)])
    position = last - ((last - (64 * gy + (lane & 63))) & (WINDOW_SLOTS - 1))
    usable = (position >= jnp.maximum(first, last - (WINDOW_SLOTS - 2))) & ((lane >> 6) == (row & 3))
    mask[...] = jnp.where(usable, 1.0, 0.0)

    turn = (l8 & 63).astype(F32)
    angle = pick(s8 & 3, [lengths[r] for r in range(4)]).astype(F32) * jnp.exp(turn * (-2.0 * math.log(10000.0) / 128))
    rotated = 2 * gy < QUERY_HEADS + KEY_VALUE_HEADS
    cosine = jnp.where(rotated, jnp.cos(angle), 1.0)
    sine = jnp.where(rotated, jnp.where(l8 < 64, -1.0, 1.0) * jnp.sin(angle), 0.0)

    v_wo[pl.ds(pl.multiple_of(192 - 64 * core, 64), 64)] = jnp.zeros((64, 384), BF16)
    loads[6].wait()

    received(ST_B, r_b)
    x = r_b[...].astype(F32)
    rows = mm(perm_c[...], (x * ag).reshape(256, 128).astype(BF16))
    left = jnp.concatenate([rows[128 * c : 128 * c + 128] for c in range(3)], axis=1).astype(BF16)
    sums = mm(left, v_wqkv[...])
    hh = (iota((128, 128), 0) >> 2) & 1
    sums = jnp.where(hh == 0, sums[:, 0:128], sums[:, 128:256])
    s_c[...] = jnp.concatenate([sums.reshape(16, 8, 128), rows[384:512].reshape(16, 8, 128)], axis=1)
    send(ST_C, "gx", s_c, r_c, True)
    x_moe[...] = (x * mg).reshape(256, 128).astype(BF16)
    for c in loads[11:12]:
        c.wait()
    for e in range(EXP_WIN):
        for u in range(2):
            w_split[e, u] = v_gu[e, :, u, :]

    received(ST_C, r_c)
    both = total(r_c)
    square = join_terms(both[8:16])
    scale = lax.rsqrt(square[:, 0:1] / MODEL_WIDTH + EPS)
    heads = both[0:8] * scale
    heads = heads * cosine + pltpu.roll(heads, 64, 1) * sine
    t_d[...] = heads.astype(BF16)
    send(ST_D, "gy", t_d, r_d, False)

    def gate_up(x_rows, out):
        rows = mm(perm_k[...], x_rows)
        rows16 = rows.astype(BF16)
        ct = (iota((128, 128), 0) & 7) >> 1
        for e in range(EXP_WIN):
            left = jnp.concatenate([rows16[(3 * e + c) * 128 : (3 * e + c) * 128 + 128] for c in range(3)], axis=1)
            halves = []
            for u in range(2):
                full = mm(left, w_split[e, u])
                halves.append(pick(ct, [full[:, 128 * k : 128 * k + 128] for k in range(4)]).reshape(16, 8, 128))
            out[:, pl.ds(16 * e, 16), :] = jnp.concatenate(halves, axis=1).astype(BF16)
        sums = rows[768:896].reshape(16, 8, 128)
        out[:, pl.ds(32, 8), :] = sums.astype(BF16)

    gate_up(x_moe[...], s_a)
    send(ST_A, "gx", s_a, r_a, True)
    for c in loads[7:11] + loads[12:13]:
        c.wait()

    received(ST_D, r_d)
    everything = r_d[...].astype(F32).reshape(256, 128).astype(BF16)
    queries = mm(sel_e[...], everything)
    q_rows[...] = queries.reshape(32, 8, 128)
    queries = queries.astype(BF16)
    q_bits[...] = queries

    def attend(part):
        groups = [lax.rem(lax.div(z, 2) + 2 + 4 * part + k, 8) for k in range(4)]
        scores = []
        for g in groups:
            lanes = pl.ds(pl.multiple_of(128 * g, 128), 128)
            scores.append(
                lax.dot_general(
                    q_bits[pl.ds(pl.multiple_of(32 * g, 32), 32)],
                    v_keys[:, :, lanes].reshape(256, 128),
                    (((1,), (1,)), ((), ())),
                    preferred_element_type=F32,
                )
            )
        score = jnp.concatenate(scores, axis=0)
        weight = jnp.exp(CAP * jnp.tanh(score * (HEAD_SIZE**-0.5 / CAP))).reshape(16, 8, 256) * mask[...]
        weight = weight.reshape(128, 256)
        weight16 = weight.astype(BF16)
        sums = []
        for k, g in enumerate(groups):
            lanes = pl.ds(pl.multiple_of(128 * g, 128), 128)
            sums.append(mm(weight16[32 * k : 32 * k + 32], v_vals[:, :, lanes].reshape(256, 128)))
        summed = jnp.concatenate(sums, axis=0)
        total1 = jnp.broadcast_to(jnp.sum(weight, axis=1, keepdims=True), (128, 128))
        total0 = pltpu.roll(total1, 4, 0)
        row, lane = iota((128, 128), 0), iota((128, 128), 1)
        low1 = total1 - total1.astype(BF16).astype(F32)
        low0 = total0 - total0.astype(BF16).astype(F32)
        free = pick((lane & 63) >> 4, [total1, low1, total0, low0])
        keep = (((row >> 2) & 1) == 0) | ((lane >> 6) == ((row >> 3) & 1))
        s_e[pl.ds(16 * part, 16)] = jnp.where(keep, summed, free).reshape(16, 8, 128).astype(BF16)

    first_chip = 2 * lax.div(z, 2) + 4

    def send_attended(k):
        chip = lax.rem(first_chip + k, 16)
        for c in range(2):
            push(ST_E, s_e.at[2 * k + c], r_e.at[gy], 2 * chip + c)

    attend(0)
    for k in (4, 3, 5, 2, 6, 1, 7, 0):
        send_attended(k)
    attend(1)
    for k in (8, 15, 9, 14, 10, 11):
        send_attended(k)
    beside = 1 - lax.rem(z, 2)
    for c in range(2):
        push(ST_E, s_e.at[24 + 2 * beside + c], r_e.at[gy], 2 * (2 * lax.div(z, 2) + beside) + c)
    own_block = 24 + 2 * lax.rem(z, 2)
    push(ST_E, s_e.at[own_block + 1 - core], r_e.at[gy], 2 * z + 1 - core)
    r_e[gy] = s_e[own_block + core]

    group = lax.div(gy, 4)
    second = lax.rem(group, 2)

    def fresh(first_block):
        tile = r_d[first_block + lax.div(group, 2)].astype(F32)
        return jnp.where((s8 >> 2) == second, tile, pltpu.roll(tile, 4, 0))

    own_query = q_rows[gy].astype(BF16).astype(F32)
    own_score = jnp.sum(own_query * fresh(24), axis=1, keepdims=True) * (HEAD_SIZE**-0.5 / CAP)
    own_weight = jnp.exp(CAP * jnp.tanh(own_score))
    own_value = own_weight.astype(BF16).astype(F32) * fresh(28)

    received(ST_E, r_e)
    tile = total(r_e)
    half = (l8 >> 6) == core
    quarter = (l8 & 63) >> 5
    den1 = jnp.sum(jnp.where(~half & (quarter == 0), tile, 0.0), axis=1, keepdims=True) * 0.0625
    den0 = jnp.sum(jnp.where(~half & (quarter == 1), tile, 0.0), axis=1, keepdims=True) * 0.0625
    den1, den0 = jnp.broadcast_to(den1, (8, 128)), jnp.broadcast_to(den0, (8, 128))
    den = jnp.where(s8 < 4, pltpu.roll(den0, 4, 0), den1) + own_weight
    attended = (tile + own_value) / den
    t_f[...] = jnp.where((s8 < 4) | half, attended, 0.0).astype(BF16)
    send(ST_F, "gx", t_f, r_f, False)

    ctile = (iota((256, 128), 0) & 7) >> 1
    received(ST_F, r_f)
    heads16 = r_f[...].astype(F32).reshape(128, 128).astype(BF16)
    cpair = (iota((128, 128), 0) & 7) >> 1

    def project(other):
        rows = mm(sel_g[pl.ds(256 * other, 256)], heads16).astype(BF16)
        sums = mm(jnp.concatenate([rows[0:128], rows[128:256]], axis=1), v_wo[...])
        return pick(cpair, [sums[:, 128 * c : 128 * c + 128] for c in range(3)]).reshape(8, 16, 128)

    s_x[...] = project(1)
    push(ST_X, s_x, r_x, 2 * z + 1 - core)
    mine = project(0)
    pltpu.make_async_copy(r_x, r_x, recv_sem.at[ST_X]).wait()
    s_g[...] = (mine + r_x[...]).astype(BF16)
    over_z(lambda far: push(ST_G, s_g.at[lax.rem(far, 8)], r_g.at[z], 2 * far + core))
    r_g[z] = s_g[low_z]
    received(ST_A, r_a)
    total_a = total(r_a)

    received(ST_G, r_g)
    both = total(r_g)
    tiles = []
    for half in range(2):
        branch = jnp.where(s8 < 6, both[8 * half : 8 * half + 8], 0.0)
        gained = branch * pg
        stream = jnp.where(s8 < 6, r_b[2 * pair + half].astype(F32), 0.0)
        branch_sums = lane_sums(
            [(0, branch * branch), (1, stream * gained), (2, gained * gained)]
            + [(3 + e, gained * rm[e]) for e in range(8)]
        )
        tiles.append(jnp.where(s8 < 6, gained * mg, split_terms(branch_sums)))
        branch_t[half] = gained
    t_j[...] = jnp.concatenate(tiles, axis=0).astype(BF16)
    over_near(lambda p: push(ST_J, t_j, r_j.at[pair], p))
    r_j[pair] = t_j[...]

    received(ST_J, r_j)
    gate_up(r_j[...].astype(F32).reshape(256, 128).astype(BF16), s_k)
    send(ST_K, "gx", s_k, r_k, True)
    received(ST_K, r_k)
    total_k = total(r_k)

    sums_a, sums_k = join_terms(total_a[32:40]), join_terms(total_k[32:40])
    post = lax.rsqrt(sums_k[:, 0:1] / MODEL_WIDTH + EPS)
    stream_square = sums_a[:, 0:1] + 2.0 * post * sums_k[:, 1:2] + post * post * sums_k[:, 2:3]
    pre = lax.rsqrt(stream_square / MODEL_WIDTH + EPS)
    logits = pre * (sums_a + post * sums_k)
    named = (l8 >= 3) & (l8 < 11)
    exponent = jnp.where(named, jnp.exp(jnp.where(named, logits, 0.0)), 0.0)
    chance = exponent / jnp.sum(exponent, axis=1, keepdims=True)
    combine = jnp.sum(jnp.where(l8 == 3 + (s8 >> 1), chance, 0.0), axis=1, keepdims=True)

    def spread(column, first):
        two = [jnp.broadcast_to(column[first + k : first + k + 1], (8, 128)) for k in range(2)]
        return jnp.where((s8 & 1) == 0, two[0], two[1])

    hidden = []
    for e in range(EXP_WIN):
        post_e, pre_e = spread(post, 2 * e), spread(pre, 2 * e)
        gate, up = (
            pre_e * (total_a[16 * e + 8 * u : 16 * e + 8 * u + 8] + post_e * total_k[16 * e + 8 * u : 16 * e + 8 * u + 8])
            for u in range(2)
        )
        bent = 0.5 * gate * (1.0 + jnp.tanh(math.sqrt(2.0 / math.pi) * (gate + 0.044715 * gate * gate * gate)))
        hidden.append(bent * up * spread(combine, 2 * e))
    t_h[...] = jnp.concatenate(hidden, axis=0).astype(BF16)
    send(ST_H, "gx", t_h, r_h, False)

    mixed = as_rows(base_t[...] + spread(post, 4) * branch_t[high])

    received(ST_H, r_h)
    hidden = r_h[...].astype(F32).reshape(256, 128).astype(BF16)
    chalf = (iota((128, 128), 0) & 7) >> 1

    def expert_sums(part):
        sums = jnp.zeros((128, 384), F32)
        for e in range(EXP_WIN):
            rows = mm(perm_l[pl.ds(1024 * part + 512 * e, 512)], hidden).astype(BF16)
            left = jnp.concatenate([rows[128 * ct : 128 * ct + 128] for ct in range(4)], axis=1)
            sums = sums + mm(left, v_wd[e])
        blocks = pick(chalf, [sums[:, 128 * c : 128 * c + 128] for c in range(3)])
        s_l[pl.ds(16 * part, 16)] = blocks.reshape(16, 8, 128).astype(BF16)

    def send_sums(k):
        chip = lax.rem(z + 5 + k, 16)
        for other in range(2):
            push(ST_L, s_l.at[2 * k + other], r_l.at[gy], 2 * chip + other)

    expert_sums(0)

    def far_chips(q, carry):
        h = lax.div(q + 1, 2)
        send_sums(3 + h * (1 - 2 * lax.rem(q, 2)))
        return carry

    lax.fori_loop(0, 7, far_chips, 0, unroll=True)
    send_sums(7)
    expert_sums(1)

    def near_chips(k, carry):
        send_sums(k)
        return carry

    lax.fori_loop(8, 11, near_chips, 0, unroll=True)
    lax.fori_loop(12, 16, near_chips, 0, unroll=True)
    push(ST_L, s_l.at[23 - core], r_l.at[gy], 2 * z + 1 - core)
    r_l[gy] = s_l[22 + core]
    for stage, dst in (
        (ST_B, r_b), (ST_C, r_c), (ST_D, r_d), (ST_E, r_e), (ST_F, r_f), (ST_G, r_g), (ST_J, r_j), (ST_A, r_a),
        (ST_K, r_k), (ST_H, r_h),
    ):
        pltpu.make_async_copy(peers_of(dst), peers_of(dst), send_sem.at[stage]).wait()
    pltpu.make_async_copy(s_x, s_x, send_sem.at[ST_X]).wait()
    received(ST_L, r_l)
    res_ref[...] = jnp.concatenate([mixed, as_rows(total(r_l))], axis=0).astype(BF16)
    pltpu.make_async_copy(peers_of(r_l), peers_of(r_l), send_sem.at[ST_L]).wait()


def local(
    residual, attn_gain, wqkv, rotated_key_cache, slot_value_cache, lengths, starts, wo, post_gain, moe_gain, router,
    expert_ids, w_gate_up, w_down,
):
    anywhere = pl.BlockSpec(memory_space=pltpu.HBM)
    scalars = pl.BlockSpec(memory_space=pltpu.SMEM)
    vmem = pltpu.VMEM
    gy_tiles = vmem((NY, 8, 128), BF16)
    gx_tiles = vmem((NX, 8, 128), BF16)
    tile = vmem((8, 128), BF16)
    pairs = vmem((16, 16, 128), BF16)
    result = pl.pallas_call(
        kernel,
        out_shape=pltpu.VMEM((4, 384), BF16),
        in_specs=[anywhere] * 5 + [scalars] * 2 + [anywhere] * 7,
        out_specs=pl.BlockSpec(memory_space=pltpu.VMEM),
        scratch_shapes=[
            vmem((2, 384), BF16), vmem((384,), F32), vmem((384,), F32), vmem((384,), F32), vmem((8, 384), BF16),
            vmem((2, 64), I32), vmem((384, 256), BF16), vmem((4, 64, 1024), BF16), vmem((4, 64, 1024), BF16),
            vmem((256, 384), BF16), vmem((2, 384, 2, 512), BF16), vmem((2, 512, 384), BF16),
            vmem((2, 2, 384, 512), BF16),
            vmem((512, 256), BF16), vmem((256, 256), BF16), vmem((512, 128), BF16), vmem((896, 256), BF16),
            vmem((2048, 256), BF16), vmem((8, 8, 128), F32), vmem((8, 256), F32), vmem((8, 128), F32),
            vmem((2, 8, 128), F32), vmem((32, 8, 128), F32), vmem((256, 128), BF16), vmem((256, 128), BF16),
            tile, gy_tiles, vmem((NX, 16, 128), F32), vmem((NX, 16, 128), F32), tile, gy_tiles, gy_tiles, gy_tiles,
            tile, gx_tiles, vmem((8, 16, 128), F32), vmem((8, 16, 128), F32), vmem((8, 16, 128), BF16), pairs,
            vmem((16, 128), BF16), pairs, vmem((NX, 40, 128), BF16), vmem((NX, 40, 128), BF16),
            vmem((NX, 40, 128), BF16), vmem((NX, 40, 128), BF16), vmem((16, 128), BF16), vmem((NX, 16, 128), BF16),
            gy_tiles, gy_tiles,
            pltpu.SemaphoreType.DMA((13,)), pltpu.SemaphoreType.DMA((12,)), pltpu.SemaphoreType.DMA((12,)),
        ],
        compiler_params=pltpu.CompilerParams(
            collective_id=0, has_side_effects=True, vmem_limit_bytes=63 * 1024 * 1024
        ),
        name="decode_step",
    )(
        residual, attn_gain, wqkv, rotated_key_cache, slot_value_cache, lengths, starts, wo,
        post_gain, moe_gain, router.T, expert_ids.T, w_gate_up, w_down,
    )
    return result[:2], result[2:]


def solution(mesh):
    return jax.shard_map(
        local,
        mesh=mesh,
        in_specs=(
            P("gy", "gx"), P("gx"), P("gx", "gy"), P("gx", "gy", None), P("gx", "gy", None), P("gx"), P("gx"),
            P("gy", "gx"), P("gx"), P("gx"), P("gx", None), P(), P(None, "gx", None, "gy"), P(None, "gy", "gx"),
        ),
        out_specs=(P("gy", "gx"), P("gy", "gx")),
        check_vma=False,
    )
```
